32 devices in a mesh: shard: 4 (over y, x), ctx: 4 (over z), tp: 2 (over core).
Axes of the slice: x: 2, y: 2, z: 4, core: 2. Of those that a mesh axis runs over, the one named last changes fastest.
Arguments:
- tokens: bfloat16 [8, 1056, 1536], P('shard', 'ctx'), may hold values from -6 to 6
- conditioning: bfloat16 [8, 130, 1536], P('shard')
- cotangent: bfloat16 [8, 1056, 1536], P('shard', 'ctx')
- piece_lengths: int32 [8, 4], P('shard'), may hold values from 192 to 257, as said below
- start_positions: int32 [8], P('shard'), may hold values from 0 to 2047
- cond_counts: int32 [8], P('shard'), may hold values from 65 to 130, as said below
- norm_gains: float32 [3, 1536], P(None, ('shard', 'ctx'))
- gains_moment: float32 [3, 1536], P(None, ('shard', 'ctx'))
- gains_square: float32 [3, 1536], P(None, ('shard', 'ctx'))
- qkv_weight: float32 [1536, 3, 1536], P(('shard', 'ctx'), None, 'tp')
- qkv_moment: float32 [1536, 3, 1536], P(('shard', 'ctx'), None, 'tp')
- qkv_square: float32 [1536, 3, 1536], P(('shard', 'ctx'), None, 'tp')
- output_weight: float32 [1536, 1536], P(('shard', 'ctx'), 'tp'), may hold values from -0.625 to 0.625
- output_moment: float32 [1536, 1536], P(('shard', 'ctx'), 'tp')
- output_square: float32 [1536, 1536], P(('shard', 'ctx'), 'tp')
- cross_query_weight: float32 [1536, 1536], P(('shard', 'ctx'), 'tp'), may hold values from -0.15625 to 0.15625
- cross_query_moment: float32 [1536, 1536], P(('shard', 'ctx'), 'tp')
- cross_query_square: float32 [1536, 1536], P(('shard', 'ctx'), 'tp')
- cross_pair_weight: float32 [1536, 2, 1536], P(('shard', 'ctx'), None, 'tp')
- cross_pair_moment: float32 [1536, 2, 1536], P(('shard', 'ctx'), None, 'tp')
- cross_pair_square: float32 [1536, 2, 1536], P(('shard', 'ctx'), None, 'tp')
- cross_out_weight: float32 [1536, 1536], P(('shard', 'ctx'), 'tp'), may hold values from -0.21875 to 0.21875
- cross_out_moment: float32 [1536, 1536], P(('shard', 'ctx'), 'tp')
- cross_out_square: float32 [1536, 1536], P(('shard', 'ctx'), 'tp')
- gate_up_weight: float32 [1536, 2, 6144], P(('shard', 'ctx'), None, 'tp')
- gate_up_moment: float32 [1536, 2, 6144], P(('shard', 'ctx'), None, 'tp')
- gate_up_square: float32 [1536, 2, 6144], P(('shard', 'ctx'), None, 'tp')
- down_weight: float32 [1536, 6144], P(('shard', 'ctx'), 'tp'), may hold values from -0.15625 to 0.15625
- down_moment: float32 [1536, 6144], P(('shard', 'ctx'), 'tp')
- down_square: float32 [1536, 6144], P(('shard', 'ctx'), 'tp')
Outputs:
- block_out: bfloat16 [8, 1056, 1536], P('shard', 'ctx')
- tokens_grad: float32 [8, 1056, 1536], P('shard', 'ctx')
- grad_norm: float32 [], replicated
- gains_moment_new: float32 [3, 1536], P(None, ('shard', 'ctx'))
- gains_square_new: float32 [3, 1536], P(None, ('shard', 'ctx'))
- gains_new: float32 [3, 1536], P(None, ('shard', 'ctx'))
- qkv_moment_new: float32 [1536, 3, 1536], P(('shard', 'ctx'), None, 'tp')
- qkv_square_new: float32 [1536, 3, 1536], P(('shard', 'ctx'), None, 'tp')
- qkv_new: float32 [1536, 3, 1536], P(('shard', 'ctx'), None, 'tp')
- output_moment_new: float32 [1536, 1536], P(('shard', 'ctx'), 'tp')
- output_square_new: float32 [1536, 1536], P(('shard', 'ctx'), 'tp')
- output_new: float32 [1536, 1536], P(('shard', 'ctx'), 'tp')
- cross_query_moment_new: float32 [1536, 1536], P(('shard', 'ctx'), 'tp')
- cross_query_square_new: float32 [1536, 1536], P(('shard', 'ctx'), 'tp')
- cross_query_new: float32 [1536, 1536], P(('shard', 'ctx'), 'tp')
- cross_pair_moment_new: float32 [1536, 2, 1536], P(('shard', 'ctx'), None, 'tp')
- cross_pair_square_new: float32 [1536, 2, 1536], P(('shard', 'ctx'), None, 'tp')
- cross_pair_new: float32 [1536, 2, 1536], P(('shard', 'ctx'), None, 'tp')
- cross_out_moment_new: float32 [1536, 1536], P(('shard', 'ctx'), 'tp')
- cross_out_square_new: float32 [1536, 1536], P(('shard', 'ctx'), 'tp')
- cross_out_new: float32 [1536, 1536], P(('shard', 'ctx'), 'tp')
- gate_up_moment_new: float32 [1536, 2, 6144], P(('shard', 'ctx'), None, 'tp')
- gate_up_square_new: float32 [1536, 2, 6144], P(('shard', 'ctx'), None, 'tp')
- gate_up_new: float32 [1536, 2, 6144], P(('shard', 'ctx'), None, 'tp')
- down_moment_new: float32 [1536, 6144], P(('shard', 'ctx'), 'tp')
- down_square_new: float32 [1536, 6144], P(('shard', 'ctx'), 'tp')
- down_new: float32 [1536, 6144], P(('shard', 'ctx'), 'tp')
The draws below stay inside these ranges and needn't reach their ends.
Inputs may be any that keep to these rules, and one draw needn't show every extreme that they name: `piece_lengths`: in each latent one piece, drawn from the seed, holds 257 tokens and the others 256 - 256 // 4 to 256; in some latent all others hold 256. A latent attends to its first cond_counts conditioning tokens; some latent has all 130.
All inputs are finite; a program needn't handle non-finite values.
Results may differ from the reference program's by a relative error of at most 0.025.
Values may be sent and summed in bfloat16 or wider, within the bound.
No kernel may reach another device: no remote copies, remote signals or barrier semaphores. Data moves between devices by JAX's collectives and lax.ppermute only.
A program may use at most 320 MiB of HBM per device.

```python
import jax
import jax.numpy as jnp
from jax import lax

D = 1536
FF = 6144
HD = 64
HEADS = 24
ROT = 32
COND = 130
PIECE = 256
CAP = 264
SEQ_DEV = 2
STEP = 7
SEQS = 8
SLOTS = 1056
N_CTX = 4


def rising(count, ratio):
    steps = jnp.arange(count, dtype=jnp.float32) / max(count - 1, 1)
    return ratio ** steps / ratio ** 0.5


def gradient_size(factor):
    return factor / float(8 * D * D + 3 * D * FF + 3 * D) ** 0.5


def first_moment(key, shape, factor):
    return 0.1111 * gradient_size(factor) * jax.random.normal(key, shape, jnp.float32)


def second_moment(key, shape, factor):
    spread = jax.random.uniform(key, shape, jnp.float32, -0.6931, 2.0794)
    return 0.001001 * gradient_size(factor) ** 2 * jnp.exp(spread)


def draw_piece_lengths(key, part):
    key = jax.random.fold_in(key, 1)
    keys = jax.random.split(key, 3)
    column = jnp.arange(N_CTX, dtype=jnp.int32)[None, :]
    row = jnp.arange(SEQS, dtype=jnp.int32)[:, None]
    base = jax.random.randint(keys[0], (SEQS, N_CTX), PIECE - PIECE // 4, PIECE + 1)
    extra = jax.random.randint(keys[1], (SEQS, 1), 0, N_CTX)
    order = jax.random.permutation(keys[2], SEQS)
    lengths = jnp.where(row == order[1], PIECE - PIECE // 4, base)
    lengths = jnp.where(row == order[0], PIECE, lengths)
    lengths = jnp.where(column == extra, PIECE + 1, lengths)
    return lengths.astype(jnp.int32)


def draw_cond_counts(key, part):
    key = jax.random.fold_in(key, 2)
    first, second = jax.random.split(key)
    counts = jax.random.randint(first, (SEQS,), COND // 2, COND + 1)
    order = jax.random.permutation(second, SEQS)
    counts = counts.at[order[0]].set(COND)
    counts = counts.at[order[1]].set(COND // 2)
    return counts.astype(jnp.int32)


def draw_conditioning(key, part):
    key = jax.random.fold_in(key, 3)
    ratio = 3.0
    base = jax.random.normal(key, (SEQS, COND, D), jnp.float32)
    return (base * rising(D, ratio)[None, None, :]).astype(jnp.bfloat16)


def draw_cotangent(key, part):
    key = jax.random.fold_in(key, 4)
    ratio = 3.0
    base = jax.random.normal(key, (SEQS, N_CTX * CAP, D), jnp.float32)
    return (base * rising(D, ratio)[None, None, :]).astype(jnp.bfloat16)


def draw_norm_gains(key, part):
    key = jax.random.fold_in(key, 5)
    ratio = 3.0
    jitter = jax.random.uniform(key, (3, D), jnp.float32, 0.8, 1.25)
    return jitter * rising(D, ratio)[None, :]


def draw_qkv_weight(key, part):
    key = jax.random.fold_in(key, 6)
    ratio = 3.0
    base = jax.random.normal(key, (D, 3, D), jnp.float32) / D ** 0.5
    lift = jnp.stack([jnp.ones((D,), jnp.float32), jnp.ones((D,), jnp.float32), rising(D, ratio)])
    return base * lift[None]


def draw_cross_pair_weight(key, part):
    key = jax.random.fold_in(key, 7)
    ratio = 3.0
    base = jax.random.normal(key, (D, 2, D), jnp.float32) / D ** 0.5
    lift = jnp.stack([jnp.ones((D,), jnp.float32), rising(D, ratio)])
    return base * lift[None]


def draw_gate_up_weight(key, part):
    key = jax.random.fold_in(key, 8)
    ratio = 3.0
    base = jax.random.normal(key, (D, 2, FF), jnp.float32) / D ** 0.5
    lift = jnp.stack([jnp.ones((FF,), jnp.float32), rising(FF, ratio)])
    return base * lift[None]


def draw_gains_moment(key, part):
    key = jax.random.fold_in(key, 20)
    return first_moment(key, (3, D), 4.0)


def draw_gains_square(key, part):
    key = jax.random.fold_in(key, 21)
    return second_moment(key, (3, D), 4.0)


def draw_qkv_moment(key, part):
    key = jax.random.fold_in(key, 22)
    return first_moment(key, (D, 3, D), 1.0)


def draw_qkv_square(key, part):
    key = jax.random.fold_in(key, 23)
    return second_moment(key, (D, 3, D), 1.0)


def draw_output_moment(key, part):
    key = jax.random.fold_in(key, 24)
    return first_moment(key, (D, D), 1.0)


def draw_output_square(key, part):
    key = jax.random.fold_in(key, 25)
    return second_moment(key, (D, D), 1.0)


def draw_cross_query_moment(key, part):
    key = jax.random.fold_in(key, 26)
    return first_moment(key, (D, D), 1.0)


def draw_cross_query_square(key, part):
    key = jax.random.fold_in(key, 27)
    return second_moment(key, (D, D), 1.0)


def draw_cross_pair_moment(key, part):
    key = jax.random.fold_in(key, 28)
    return first_moment(key, (D, 2, D), 1.0)


def draw_cross_pair_square(key, part):
    key = jax.random.fold_in(key, 29)
    return second_moment(key, (D, 2, D), 1.0)


def draw_cross_out_moment(key, part):
    key = jax.random.fold_in(key, 30)
    return first_moment(key, (D, D), 1.0)


def draw_cross_out_square(key, part):
    key = jax.random.fold_in(key, 31)
    return second_moment(key, (D, D), 1.0)


def draw_gate_up_moment(key, part):
    key = jax.random.fold_in(key, 32)
    return first_moment(key, (D, 2, FF), 1.0)


def draw_gate_up_square(key, part):
    key = jax.random.fold_in(key, 33)
    return second_moment(key, (D, 2, FF), 1.0)


def draw_down_moment(key, part):
    key = jax.random.fold_in(key, 34)
    return first_moment(key, (D, FF), 1.0)


def draw_down_square(key, part):
    key = jax.random.fold_in(key, 35)
    return second_moment(key, (D, FF), 1.0)


def touch_ends(result, rng, low, largest):
    shape = result.shape
    place = [jax.random.randint(jax.random.fold_in(rng, axis), (), 0, shape[axis]) for axis in range(len(shape))]
    result = result.at[tuple(place)].set(low)
    longest = shape.index(max(shape))
    place[longest] = (place[longest] + 1) % shape[longest]
    return result.at[tuple(place)].set(largest)


def level_of(rng, dims, shards, smallest, top_value):
    factor_of = 1.0
    for position, parts in shards:
        heights = jax.random.uniform(jax.random.fold_in(jax.random.fold_in(rng, 6), position), (parts,), jnp.float32, smallest / len(shards), top_value / len(shards))
        factor_of = factor_of * jnp.repeat(jnp.exp(heights), dims[position] // parts).reshape((-1,) + (1,) * (len(dims) - 1 - position))
    return factor_of


def normal_values(own_key, extent, width, bound, shards=(), kind=jnp.bfloat16):
    factor_of = level_of(own_key, extent, shards, -0.22, 0.18) if shards else 1.0
    entries = jax.random.normal(own_key, extent, jnp.float32) * width * factor_of
    return jnp.minimum(jnp.maximum(entries, -bound), bound).astype(kind)


def setup_inputs(seed: int = 0) -> dict:
    streams_of = jax.random.split(jax.random.key(seed), 31)
    return {
        "tokens": normal_values(streams_of[0], (SEQS, SLOTS, D), 1.0, 6.0, ((0, 4), (1, 4))),
        "conditioning": draw_conditioning(jax.random.fold_in(streams_of[30], 71), 0),
        "cotangent": draw_cotangent(jax.random.fold_in(streams_of[30], 71), 0),
        "piece_lengths": draw_piece_lengths(jax.random.fold_in(streams_of[30], 71), 0),
        "start_positions": touch_ends(jax.random.randint(streams_of[4], (SEQS,), 0, 2048), jax.random.fold_in(streams_of[4], 1), 0, 2047).astype(jnp.int32),
        "cond_counts": draw_cond_counts(jax.random.fold_in(streams_of[30], 71), 0),
        "norm_gains": draw_norm_gains(jax.random.fold_in(streams_of[30], 71), 0),
        "gains_moment": draw_gains_moment(jax.random.fold_in(streams_of[30], 71), 0),
        "gains_square": draw_gains_square(jax.random.fold_in(streams_of[30], 71), 0),
        "qkv_weight": draw_qkv_weight(jax.random.fold_in(streams_of[30], 71), 0),
        "qkv_moment": draw_qkv_moment(jax.random.fold_in(streams_of[30], 71), 0),
        "qkv_square": draw_qkv_square(jax.random.fold_in(streams_of[30], 71), 0),
        "output_weight": normal_values(streams_of[12], (D, D), (D // 16) ** -0.5, 0.625, ((0, 16), (1, 2)), jnp.float32),
        "output_moment": draw_output_moment(jax.random.fold_in(streams_of[30], 71), 0),
        "output_square": draw_output_square(jax.random.fold_in(streams_of[30], 71), 0),
        "cross_query_weight": normal_values(streams_of[15], (D, D), D ** -0.5, 0.15625, ((0, 16), (1, 2)), jnp.float32),
        "cross_query_moment": draw_cross_query_moment(jax.random.fold_in(streams_of[30], 71), 0),
        "cross_query_square": draw_cross_query_square(jax.random.fold_in(streams_of[30], 71), 0),
        "cross_pair_weight": draw_cross_pair_weight(jax.random.fold_in(streams_of[30], 71), 0),
        "cross_pair_moment": draw_cross_pair_moment(jax.random.fold_in(streams_of[30], 71), 0),
        "cross_pair_square": draw_cross_pair_square(jax.random.fold_in(streams_of[30], 71), 0),
        "cross_out_weight": normal_values(streams_of[21], (D, D), (D // 2) ** -0.5, 0.21875, ((0, 16), (1, 2)), jnp.float32),
        "cross_out_moment": draw_cross_out_moment(jax.random.fold_in(streams_of[30], 71), 0),
        "cross_out_square": draw_cross_out_square(jax.random.fold_in(streams_of[30], 71), 0),
        "gate_up_weight": draw_gate_up_weight(jax.random.fold_in(streams_of[30], 71), 0),
        "gate_up_moment": draw_gate_up_moment(jax.random.fold_in(streams_of[30], 71), 0),
        "gate_up_square": draw_gate_up_square(jax.random.fold_in(streams_of[30], 71), 0),
        "down_weight": normal_values(streams_of[27], (D, FF), (FF // 4) ** -0.5, 0.15625, ((0, 16), (1, 2)), jnp.float32),
        "down_moment": draw_down_moment(jax.random.fold_in(streams_of[30], 71), 0),
        "down_square": draw_down_square(jax.random.fold_in(streams_of[30], 71), 0),
    }


highest = lax.Precision.HIGHEST
norm_eps = 1e-05
clip_norm = 1.0
beta_first = 0.9
beta_second = 0.999
learn_rate = 0.03
gain_rate = 0.75
weight_decay = 0.01
adam_eps = 1e-08
masked_score = -1e+30

@jax.custom_vjp
def low(v):
    return lax.optimization_barrier(v.astype(jnp.bfloat16)).astype(jnp.float32)

@jax.custom_vjp
def low_back(v):
    return v

def low_keep(v):
    return (low(v), None)

def low_pass(kept, grad):
    return (grad,)

def back_keep(v):
    return (v, None)

def back_low(kept, grad):
    return (low(grad),)
low.defvjp(low_keep, low_pass)
low_back.defvjp(back_keep, back_low)

def frequencies(rotary):
    return 10000.0 ** (-jnp.arange(rotary // 2, dtype=jnp.float32) * 2.0 / rotary)

def rotate(heads, cosine, sine, rotary):
    half = rotary // 2
    first = heads[..., :half]
    second = heads[..., half:rotary]
    cosine = cosine[..., None, :]
    sine = sine[..., None, :]
    return jnp.concatenate([first * cosine - second * sine, second * cosine + first * sine, heads[..., rotary:]], axis=-1)

def layer_norm(rows, gain):
    middle = lax.optimization_barrier(jnp.mean(rows, axis=-1, keepdims=True))
    centred = rows - middle
    variance = lax.optimization_barrier(jnp.mean(centred * centred, axis=-1, keepdims=True))
    return centred * lax.rsqrt(variance + norm_eps) * gain

def attend(items):
    queries, keys, values, key_mask = items
    scores = jnp.einsum('qhd,khd->hqk', queries, keys, precision=highest) * HD ** (-0.5)
    scores = low_back(scores)
    scores = jnp.where(key_mask[None, None, :], scores, masked_score)
    peak = lax.optimization_barrier(jnp.max(scores, axis=-1, keepdims=True))
    weights = jnp.exp(scores - peak)
    total = lax.optimization_barrier(jnp.sum(weights, axis=-1))
    mixed = jnp.einsum('hqk,khd->qhd', low(weights), values, precision=highest)
    return mixed / jnp.transpose(total)[..., None]

def block(weights, rows, cond, lengths, starts, counts):
    gains, qkv, output, query, pair, cross, gate_up, down = weights
    seqs = rows.shape[0]
    slots = N_CTX * CAP
    slot = jnp.arange(CAP, dtype=jnp.int32)
    offsets = jnp.cumsum(lengths, axis=1) - lengths
    positions = (starts[:, None, None] + offsets[:, :, None] + slot[None, None, :]).reshape(seqs, slots)
    key_valid = (slot[None, None, :] < lengths[:, :, None]).reshape(seqs, slots)
    angles = positions.astype(jnp.float32)[..., None] * frequencies(ROT)
    cosine = jnp.cos(angles)
    sine = jnp.sin(angles)
    normed1 = low(layer_norm(rows, gains[0]))
    projected = low_back(jnp.einsum('snd,dcf->sncf', normed1, qkv, precision=highest)).reshape(seqs, slots, 3, HEADS, HD)
    queries = low(rotate(projected[:, :, 0], cosine, sine, ROT))
    keys = low(rotate(projected[:, :, 1], cosine, sine, ROT))
    values = low(projected[:, :, 2])
    mixed = lax.map(jax.checkpoint(attend), (queries, keys, values, key_valid))
    mixed = low(low_back(mixed)).reshape(seqs, slots, D)
    first = rows + low_back(jnp.einsum('snf,df->snd', mixed, output, precision=highest))
    normed2 = low(layer_norm(first, gains[1]))
    cross_queries = low(low_back(jnp.einsum('snd,df->snf', normed2, query, precision=highest))).reshape(seqs, slots, HEADS, HD)
    pairs = low_back(jnp.einsum('std,dcf->stcf', cond, pair, precision=highest)).reshape(seqs, COND, 2, HEADS, HD)
    cross_keys = low(pairs[:, :, 0])
    cross_values = low(pairs[:, :, 1])
    cond_valid = jnp.arange(COND, dtype=jnp.int32)[None, :] < counts[:, None]
    cross_mixed = lax.map(jax.checkpoint(attend), (cross_queries, cross_keys, cross_values, cond_valid))
    cross_mixed = low(low_back(cross_mixed)).reshape(seqs, slots, D)
    second = first + low_back(jnp.einsum('snf,df->snd', cross_mixed, cross, precision=highest))
    normed3 = low(layer_norm(second, gains[2]))
    gated = low_back(jnp.einsum('snd,dcf->sncf', normed3, gate_up, precision=highest))
    hidden = low(jax.nn.silu(gated[:, :, 0]) * gated[:, :, 1])
    return second + low_back(jnp.einsum('snf,df->snd', hidden, down, precision=highest))

def forward(weights, rows, cond, lengths, starts, counts):
    lowered = tuple((low(weight) for weight in weights))
    groups = SEQS // SEQ_DEV

    def split(value):
        return value.reshape((groups, SEQ_DEV) + value.shape[1:])

    def step(carry, group):
        rows_group, cond_group, lengths_group, starts_group, counts_group = group
        return (carry, block(lowered, rows_group, cond_group, lengths_group, starts_group, counts_group))
    carry, outputs = lax.scan(jax.checkpoint(step), jnp.zeros((), jnp.float32), (split(rows), split(cond), split(lengths), split(starts), split(counts)))
    return outputs.reshape(rows.shape)

def adam_step(weight, moment, square, grad, scale, decay, rate):
    grad = grad * scale
    moment_new = beta_first * moment + (1.0 - beta_first) * grad
    square_new = beta_second * square + (1.0 - beta_second) * grad * grad
    moment_hat = moment_new / (1.0 - beta_first ** STEP)
    square_hat = square_new / (1.0 - beta_second ** STEP)
    weight_new = weight - rate * (moment_hat / (jnp.sqrt(square_hat) + adam_eps) + decay * weight)
    return (moment_new, square_new, weight_new)

def reference(tokens, conditioning, cotangent, piece_lengths, start_positions, cond_counts, norm_gains, gains_moment, gains_square, qkv_weight, qkv_moment, qkv_square, output_weight, output_moment, output_square, cross_query_weight, cross_query_moment, cross_query_square, cross_pair_weight, cross_pair_moment, cross_pair_square, cross_out_weight, cross_out_moment, cross_out_square, gate_up_weight, gate_up_moment, gate_up_square, down_weight, down_moment, down_square):
    weights = (norm_gains, qkv_weight, output_weight, cross_query_weight, cross_pair_weight, cross_out_weight, gate_up_weight, down_weight)
    cond = conditioning.astype(jnp.float32)
    rows = tokens.astype(jnp.float32)

    def apply(weights_in, rows_in):
        return forward(weights_in, rows_in, cond, piece_lengths, start_positions, cond_counts)
    outputs, pullback = jax.vjp(apply, weights, rows)
    slot = jnp.arange(CAP, dtype=jnp.int32)
    valid = (slot[None, None, :] < piece_lengths[:, :, None]).reshape(SEQS, N_CTX * CAP, 1).astype(jnp.float32)
    grads, tokens_grad = pullback(cotangent.astype(jnp.float32) * valid)
    squares = jnp.zeros((), jnp.float32)
    for grad in grads:
        squares = squares + jnp.sum(grad * grad)
    grad_norm = jnp.sqrt(squares)
    scale = clip_norm / jnp.maximum(grad_norm, clip_norm)
    gains_m, gains_v, gains_w = adam_step(norm_gains, gains_moment, gains_square, grads[0], scale, 0.0, gain_rate)
    qkv_m, qkv_v, qkv_w = adam_step(qkv_weight, qkv_moment, qkv_square, grads[1], scale, weight_decay, learn_rate)
    output_m, output_v, output_w = adam_step(output_weight, output_moment, output_square, grads[2], scale, weight_decay, learn_rate)
    query_m, query_v, query_w = adam_step(cross_query_weight, cross_query_moment, cross_query_square, grads[3], scale, weight_decay, learn_rate)
    pair_m, pair_v, pair_w = adam_step(cross_pair_weight, cross_pair_moment, cross_pair_square, grads[4], scale, weight_decay, learn_rate)
    cross_m, cross_v, cross_w = adam_step(cross_out_weight, cross_out_moment, cross_out_square, grads[5], scale, weight_decay, learn_rate)
    gate_m, gate_v, gate_w = adam_step(gate_up_weight, gate_up_moment, gate_up_square, grads[6], scale, weight_decay, learn_rate)
    down_m, down_v, down_w = adam_step(down_weight, down_moment, down_square, grads[7], scale, weight_decay, learn_rate)
    return (outputs.astype(jnp.bfloat16), tokens_grad, grad_norm, gains_m, gains_v, gains_w, qkv_m, qkv_v, qkv_w, output_m, output_v, output_w, query_m, query_v, query_w, pair_m, pair_v, pair_w, cross_m, cross_v, cross_w, gate_m, gate_v, gate_w, down_m, down_v, down_w)
```

```python
import functools

import jax
import jax.numpy as jnp
from jax import lax
from jax.experimental import pallas as pl
from jax.experimental.pallas import tpu as pltpu
from jax.sharding import PartitionSpec as P

HD = 64
ROT = 32
STEP = 7
LANES = 128


norm_eps = 1e-05
clip_norm = 1.0
beta_first = 0.9
beta_second = 0.999
learn_rate = 0.03
gain_rate = 0.75
weight_decay = 0.01
adam_eps = 1e-08
masked_score = -1e30
bf = jnp.bfloat16
fl = jnp.float32
MIB = 1024 * 1024


def params(mib):
    return pltpu.CompilerParams(vmem_limit_bytes=mib * MIB)


def whole(shape):
    return pl.BlockSpec(shape, lambda *index: (0,) * len(shape))


def matmul_t(left, right):
    return lax.dot_general(
        left, right, (((1,), (1,)), ((), ())), preferred_element_type=jnp.float32
    )


def matmul(left, right):
    return jnp.dot(left, right, preferred_element_type=jnp.float32)


def contract_rows(left, right):
    return lax.dot_general(
        left, right, (((0,), (0,)), ((), ())), preferred_element_type=jnp.float32
    )


def flip(block):
    return block.astype(fl).T


def norm_parts(rows):
    middle = jnp.mean(rows, axis=-1, keepdims=True)
    centred = rows - middle
    variance = jnp.mean(centred * centred, axis=-1, keepdims=True)
    inverse = lax.rsqrt(variance + norm_eps)
    return (centred * inverse, inverse)


def norm_back(grad_out, plain, inverse, gain):
    scaled = grad_out * gain
    term_mean = jnp.mean(scaled, axis=-1, keepdims=True)
    term_along = jnp.mean(scaled * plain, axis=-1, keepdims=True)
    return (inverse * (scaled - term_mean - plain * term_along), jnp.sum(grad_out * plain, axis=0))


def turn(lanes, cosine, sine_up, sine_down):
    return (
        lanes * cosine
        + pltpu.roll(lanes, ROT // 2, 1) * sine_up
        + pltpu.roll(lanes, LANES - ROT // 2, 1) * sine_down
    )


def project_kernel(
    wide, scale, x_ref, gain_ref, w_ref, cos_ref, up_ref, down_ref, a_ref, qkv_ref
):
    plain, _ = norm_parts(x_ref[...].astype(fl))
    rows = (plain * gain_ref[...]).astype(bf)
    a_ref[...] = rows
    projected = matmul(rows, w_ref[...])
    cosine, up, down = cos_ref[...], up_ref[...], down_ref[...]
    for start in range(0, 2 * wide, LANES):
        turned = turn(projected[:, start : start + LANES], cosine, up, down)
        if start < wide:
            turned = turned * scale
        qkv_ref[:, start : start + LANES] = turned.astype(bf)
    qkv_ref[:, 2 * wide :] = projected[:, 2 * wide :].astype(bf)


def project(x, gain, weight, tables, scale, block):
    rows, width = x.shape
    wide = weight.shape[1] // 3
    cosine, up, down = tables
    by_rows = lambda lanes: pl.BlockSpec((block, lanes), lambda i: (i, 0))
    return pl.pallas_call(
        functools.partial(project_kernel, wide, scale),
        grid=(rows // block,),
        in_specs=[
            by_rows(width),
            whole((1, width)),
            whole(weight.shape),
            by_rows(LANES),
            by_rows(LANES),
            by_rows(LANES),
        ],
        out_specs=[by_rows(width), by_rows(3 * wide)],
        out_shape=[
            jax.ShapeDtypeStruct((rows, width), bf),
            jax.ShapeDtypeStruct((rows, 3 * wide), bf),
        ],
        compiler_params=params(48),
        cost_estimate=pl.CostEstimate(
            flops=2 * rows * width * 3 * wide,
            bytes_accessed=4 * rows * width + 2 * rows * 3 * wide,
            transcendentals=0,
        ),
        name="project",
    )(x, gain, weight, cosine, up, down)


def attend_kernel(heads, wide, block, qkv_ref, mask_ref, o_ref, lse_ref):
    mask = mask_ref[:, 0:1] > 0.5
    total = qkv_ref.shape[0]
    if heads * HD < wide:
        o_ref[:, heads * HD :] = jnp.zeros((total, wide - heads * HD), bf)
    for h in range(heads):
        low, high = h * HD, (h + 1) * HD
        keys = qkv_ref[:, wide + low : wide + high]
        values_t = flip(qkv_ref[:, 2 * wide + low : 2 * wide + high]).astype(bf)
        for b in range(total // block):
            queries = qkv_ref[b * block : (b + 1) * block, low:high]
            scores = jnp.where(mask, matmul_t(keys, queries), masked_score)
            peak = jnp.max(scores, axis=0, keepdims=True)
            weights = jnp.exp(scores - peak)
            sums = jnp.sum(weights, axis=0, keepdims=True)
            mixed = matmul(values_t, weights.astype(bf)) / sums
            o_ref[b * block : (b + 1) * block, low:high] = mixed.T.astype(bf)
            spot = h * (total // block) + b
            lse_ref[0, spot : spot + 1, :] = peak + jnp.log(sums)


def attend(qkv, mask, latents, heads, block):
    rows, lanes = qkv.shape
    wide = lanes // 3
    total = rows // latents
    spots = heads * (total // block)
    spots_up = -(-spots // 8) * 8
    return pl.pallas_call(
        functools.partial(attend_kernel, heads, wide, block),
        grid=(latents,),
        in_specs=[
            pl.BlockSpec((total, lanes), lambda i: (i, 0)),
            pl.BlockSpec((total, LANES), lambda i: (i, 0)),
        ],
        out_specs=[
            pl.BlockSpec((total, wide), lambda i: (i, 0)),
            pl.BlockSpec((1, spots_up, block), lambda i: (i, 0, 0)),
        ],
        out_shape=[
            jax.ShapeDtypeStruct((rows, wide), bf),
            jax.ShapeDtypeStruct((latents, spots_up, block), fl),
        ],
        compiler_params=params(48),
        cost_estimate=pl.CostEstimate(
            flops=latents * heads * total * total * 16 * HD,
            bytes_accessed=rows * 4 * wide * 2,
            transcendentals=latents * heads * total * total,
        ),
        name="attend",
    )(qkv, mask)


def attend_back_kernel(
    heads, wide, block, scale, qkv_ref, do_ref, o_ref, lse_ref, mask_ref, cos_ref, up_ref, down_ref,
    out_ref, work_ref,
):
    mask = mask_ref[:, 0:1] > 0.5
    total = qkv_ref.shape[0]
    ones = jnp.ones((8, HD), fl)
    if heads * HD < wide:
        for part in range(3):
            work_ref[:, part * wide + heads * HD : (part + 1) * wide] = jnp.zeros(
                (total, wide - heads * HD), fl
            )
    for h in range(heads):
        low, high = h * HD, (h + 1) * HD
        keys = qkv_ref[:, wide + low : wide + high]
        keys_t = flip(keys).astype(bf)
        values = qkv_ref[:, 2 * wide + low : 2 * wide + high]
        grad_keys = jnp.zeros((total, HD), fl)
        grad_values = jnp.zeros((total, HD), fl)
        for b in range(total // block):
            queries = qkv_ref[b * block : (b + 1) * block, low:high]
            grads = do_ref[b * block : (b + 1) * block, low:high]
            mixed = o_ref[b * block : (b + 1) * block, low:high]
            spot = h * (total // block) + b
            scores = jnp.where(mask, matmul_t(keys, queries), masked_score)
            probs = jnp.exp(scores - lse_ref[0, spot : spot + 1, :])
            delta = lax.dot_general(
                ones,
                grads.astype(fl) * mixed.astype(fl),
                (((1,), (1,)), ((), ())),
                precision=lax.Precision.HIGHEST,
                preferred_element_type=fl,
            )[0:1]
            grad_scores = (probs * (matmul_t(values, grads) - delta)).astype(bf)
            grad_values += matmul(probs.astype(bf), grads)
            grad_keys += matmul(grad_scores, queries)
            grad_queries = matmul(keys_t, grad_scores) * scale
            work_ref[b * block : (b + 1) * block, low:high] = grad_queries.T
        work_ref[:, wide + low : wide + high] = grad_keys
        work_ref[:, 2 * wide + low : 2 * wide + high] = grad_values
    cosine, up, down = cos_ref[...], -up_ref[...], -down_ref[...]
    for start in range(0, 2 * wide, LANES):
        out_ref[:, start : start + LANES] = turn(
            work_ref[:, start : start + LANES], cosine, up, down
        ).astype(bf)
    out_ref[:, 2 * wide :] = work_ref[:, 2 * wide :].astype(bf)


def attend_back(qkv, grads, mixed, lse, mask, tables, latents, heads, block, scale):
    rows, lanes = qkv.shape
    wide = lanes // 3
    total = rows // latents
    by_latent = lambda n: pl.BlockSpec((total, n), lambda i: (i, 0))
    return pl.pallas_call(
        functools.partial(attend_back_kernel, heads, wide, block, scale),
        grid=(latents,),
        in_specs=[
            by_latent(lanes),
            by_latent(wide),
            by_latent(wide),
            pl.BlockSpec((1,) + lse.shape[1:], lambda i: (i, 0, 0)),
            by_latent(LANES),
            by_latent(LANES),
            by_latent(LANES),
            by_latent(LANES),
        ],
        out_specs=by_latent(lanes),
        out_shape=jax.ShapeDtypeStruct((rows, lanes), bf),
        scratch_shapes=[pltpu.VMEM((total, lanes), fl)],
        compiler_params=params(56),
        cost_estimate=pl.CostEstimate(
            flops=latents * heads * total * total * 40 * HD,
            bytes_accessed=rows * 10 * wide * 2,
            transcendentals=latents * heads * total * total,
        ),
        name="attend_back",
    )(qkv, grads, mixed, lse, mask, *tables)


def cross_kernel(heads, scale, q_ref, kv_ref, mask_ref, o_ref, lse_ref):
    mask = mask_ref[0, :, 0:1] > 0.5
    wide = heads * HD
    for first in range(0, heads, 2):
        pair = []
        for h in (first, first + 1):
            low, high = h * HD, (h + 1) * HD
            keys = kv_ref[0, :, low:high]
            values_t = flip(kv_ref[0, :, wide + low : wide + high]).astype(bf)
            scores = jnp.where(mask, matmul_t(keys, q_ref[0, :, low:high]) * scale, masked_score)
            peak = jnp.max(scores, axis=0, keepdims=True)
            weights = jnp.exp(scores - peak)
            sums = jnp.sum(weights, axis=0, keepdims=True)
            pair.append(matmul(values_t, weights.astype(bf)) / sums)
            lse_ref[0, h : h + 1, :] = peak + jnp.log(sums)
        o_ref[0, :, first * HD : (first + 2) * HD] = (
            jnp.concatenate(pair, axis=0).T.astype(bf)
        )


def cross(queries, pairs, mask, scale):
    latents, rows, wide = queries.shape
    heads = wide // HD
    heads_up = -(-heads // 8) * 8
    one = lambda shape: pl.BlockSpec((1,) + shape, lambda i: (i, 0, 0))
    return pl.pallas_call(
        functools.partial(cross_kernel, heads, scale),
        grid=(latents,),
        in_specs=[one((rows, wide)), one(pairs.shape[1:]), one(mask.shape[1:])],
        out_specs=[one((rows, wide)), one((heads_up, rows))],
        out_shape=[
            jax.ShapeDtypeStruct((latents, rows, wide), bf),
            jax.ShapeDtypeStruct((latents, heads_up, rows), fl),
        ],
        compiler_params=params(32),
        cost_estimate=pl.CostEstimate(
            flops=latents * heads * rows * 256 * 16 * HD,
            bytes_accessed=8 * latents * rows * wide,
            transcendentals=latents * heads * rows * 144,
        ),
        name="cross",
    )(queries, pairs, mask)


def cross_back_kernel(
    heads, scale, q_ref, kv_ref, do_ref, o_ref, lse_ref, mask_ref, dq_ref, dkv_ref
):
    mask = mask_ref[0, :, 0:1] > 0.5
    wide = heads * HD
    ones = jnp.ones((8, HD), fl)
    for first in range(0, heads, 2):
        pair = []
        grad_keys = []
        grad_values = []
        for h in (first, first + 1):
            low, high = h * HD, (h + 1) * HD
            keys = kv_ref[0, :, low:high]
            keys_t = flip(keys).astype(bf)
            values = kv_ref[0, :, wide + low : wide + high]
            queries = q_ref[0, :, low:high]
            grads = do_ref[0, :, low:high]
            scores = jnp.where(mask, matmul_t(keys, queries) * scale, masked_score)
            probs = jnp.exp(scores - lse_ref[0, h : h + 1, :])
            delta = lax.dot_general(
                ones,
                grads.astype(fl) * o_ref[0, :, low:high].astype(fl),
                (((1,), (1,)), ((), ())),
                precision=lax.Precision.HIGHEST,
                preferred_element_type=fl,
            )[0:1]
            grad_scores = (probs * (matmul_t(values, grads) - delta)).astype(bf)
            grad_values.append(matmul(probs.astype(bf), grads))
            grad_keys.append(matmul(grad_scores, queries) * scale)
            pair.append(matmul(keys_t, grad_scores) * scale)
        low, high = first * HD, (first + 2) * HD
        dq_ref[0, :, low:high] = jnp.concatenate(pair, axis=0).T.astype(bf)
        dkv_ref[0, :, low:high] = jnp.concatenate(grad_keys, axis=1).astype(bf)
        dkv_ref[0, :, wide + low : wide + high] = jnp.concatenate(grad_values, axis=1).astype(bf)


def cross_back(queries, pairs, grads, mixed, lse, mask, scale):
    latents, rows, wide = queries.shape
    heads = wide // HD
    one = lambda shape: pl.BlockSpec((1,) + shape, lambda i: (i, 0, 0))
    return pl.pallas_call(
        functools.partial(cross_back_kernel, heads, scale),
        grid=(latents,),
        in_specs=[
            one((rows, wide)),
            one(pairs.shape[1:]),
            one((rows, wide)),
            one((rows, wide)),
            one(lse.shape[1:]),
            one(mask.shape[1:]),
        ],
        out_specs=[one((rows, wide)), one(pairs.shape[1:])],
        out_shape=[
            jax.ShapeDtypeStruct(queries.shape, bf),
            jax.ShapeDtypeStruct(pairs.shape, bf),
        ],
        compiler_params=params(32),
        cost_estimate=pl.CostEstimate(
            flops=latents * heads * rows * 256 * 40 * HD,
            bytes_accessed=12 * latents * rows * wide,
            transcendentals=latents * heads * rows * 144,
        ),
        name="cross_back",
    )(queries, pairs, grads, mixed, lse, mask)


def mlp_kernel(a_ref, dy_ref, w_ref, h_ref, dgu_ref, out_ref, da_ref):
    units = h_ref.shape[1]
    rows = a_ref[...]
    gate = matmul(rows, w_ref[:, :units])
    upward = matmul(rows, w_ref[:, units : 2 * units])
    sigmoid = jax.nn.sigmoid(gate)
    activated = gate * sigmoid
    hidden = (activated * upward).astype(bf)
    h_ref[...] = hidden
    grad_hidden = matmul(dy_ref[...], w_ref[:, 2 * units :])
    grad_gate = (grad_hidden * upward * sigmoid * (1.0 + gate * (1.0 - sigmoid))).astype(bf)
    grad_up = (grad_hidden * activated).astype(bf)
    dgu_ref[:, :units] = grad_gate
    dgu_ref[:, units:] = grad_up
    da_ref[...] = (
        matmul_t(grad_gate, w_ref[:, :units]) + matmul_t(grad_up, w_ref[:, units : 2 * units])
    ).astype(bf)
    out_ref[...] = matmul_t(hidden, w_ref[:, 2 * units :]).astype(bf)


def mlp(rows, grads, weight, block):
    count, width = rows.shape
    units = weight.shape[1] // 3
    by_rows = lambda lanes: pl.BlockSpec((block, lanes), lambda i: (i, 0))
    return pl.pallas_call(
        mlp_kernel,
        grid=(count // block,),
        in_specs=[by_rows(width), by_rows(width), whole(weight.shape)],
        out_specs=[by_rows(units), by_rows(2 * units), by_rows(width), by_rows(width)],
        out_shape=[
            jax.ShapeDtypeStruct((count, units), bf),
            jax.ShapeDtypeStruct((count, 2 * units), bf),
            jax.ShapeDtypeStruct((count, width), bf),
            jax.ShapeDtypeStruct((count, width), bf),
        ],
        compiler_params=params(56),
        cost_estimate=pl.CostEstimate(
            flops=12 * count * width * units,
            bytes_accessed=2 * count * (4 * width + 3 * units) + 6 * width * units,
            transcendentals=count * units,
        ),
        name="mlp",
    )(rows, grads, weight)


def swap(value):
    return lax.ppermute(value, "tp", [(0, 1), (1, 0)])


def ring_shift(value, by):
    size = lax.axis_size("ctx")
    return lax.ppermute(value, "ctx", [(i, (i - by) % size) for i in range(size)])


def cross_over(value, bits):
    size = lax.axis_size("shard")
    return lax.ppermute(value, "shard", [(i, i ^ bits) for i in range(size)])


def ring_gather(own):
    if lax.axis_size("ctx") != 4:
        return [own] + [ring_shift(own, r) for r in range(1, lax.axis_size("ctx"))]
    half = own.shape[-1] // 2
    after = ring_shift(own, 1)
    before = ring_shift(own, -1)
    far = jnp.concatenate(
        [ring_shift(after[:, :half], 1), ring_shift(before[:, half:], -1)], axis=-1
    )
    return [own, after, far, before]


def ring_scatter(parts):
    if lax.axis_size("ctx") != 4:
        total = parts[0].astype(fl)
        for r in range(1, len(parts)):
            total = total + ring_shift(parts[r], -r).astype(fl)
        return total
    half = parts[0].shape[-1] // 2
    by_after = ring_shift(parts[2][:, :half], -1)
    by_before = ring_shift(parts[2][:, half:], 1)
    to_after = jnp.concatenate([parts[1][:, :half] + by_after, parts[1][:, half:]], axis=-1)
    to_before = jnp.concatenate([parts[3][:, :half], parts[3][:, half:] + by_before], axis=-1)
    return (
        parts[0].astype(fl)
        + ring_shift(to_after, -1).astype(fl)
        + ring_shift(to_before, 1).astype(fl)
    )


def square_gather(own):
    size = lax.axis_size("shard")
    if size != 4:
        every = lax.all_gather(own, "shard", axis=0, tiled=False)
        return [every[i] for i in range(size)]
    half = own.shape[-1] // 2
    one = cross_over(own, 1)
    two = cross_over(own, 2)
    three = jnp.concatenate([cross_over(two[:, :half], 1), cross_over(one[:, half:], 2)], axis=-1)
    return [own, one, two, three]


def square_scatter(parts):
    size = lax.axis_size("shard")
    if size != 4:
        return lax.psum_scatter(
            jnp.concatenate(parts, axis=0), "shard", scatter_dimension=0, tiled=True
        ).astype(fl)
    half = parts[0].shape[-1] // 2
    by_one = cross_over(parts[3][:, :half], 1)
    by_two = cross_over(parts[3][:, half:], 2)
    to_two = jnp.concatenate([parts[2][:, :half] + by_one, parts[2][:, half:]], axis=-1)
    to_one = jnp.concatenate([parts[1][:, :half], parts[1][:, half:] + by_two], axis=-1)
    return (
        parts[0].astype(fl)
        + cross_over(to_one, 1).astype(fl)
        + cross_over(to_two, 2).astype(fl)
    )


def total_over_all(value):
    for axis in ("tp", "shard", "ctx"):
        size = lax.axis_size(axis)
        bit = 1
        while bit < size:
            value = value + lax.ppermute(value, axis, [(i, i ^ bit) for i in range(size)])
            bit *= 2
    return value


def adam_step(weight, moment, square, grad, scale, decay, rate):
    grad = grad * scale
    moment_new = beta_first * moment + (1.0 - beta_first) * grad
    square_new = beta_second * square + (1.0 - beta_second) * grad * grad
    moment_hat = moment_new / (1.0 - beta_first**STEP)
    square_hat = square_new / (1.0 - beta_second**STEP)
    weight_new = weight - rate * (moment_hat / (jnp.sqrt(square_hat) + adam_eps) + decay * weight)
    return (moment_new, square_new, weight_new)


def rotary_tables(positions):
    lane = jnp.arange(LANES, dtype=jnp.int32) % HD
    step = (lane % (ROT // 2)).astype(fl) * 2.0 / ROT
    frequency = jnp.where(lane < ROT, 10000.0 ** (-step), 0.0)
    angles = positions.astype(fl)[:, None] * frequency[None, :]
    sine = jnp.sin(angles)
    up = jnp.where((lane >= ROT // 2) & (lane < ROT), sine, 0.0)
    down = jnp.where(lane < ROT // 2, -sine, 0.0)
    return (jnp.cos(angles), up, down)


def local(
    tokens,
    conditioning,
    cotangent,
    piece_lengths,
    start_positions,
    cond_counts,
    norm_gains,
    gains_moment,
    gains_square,
    qkv_weight,
    qkv_moment,
    qkv_square,
    output_weight,
    output_moment,
    output_square,
    cross_query_weight,
    cross_query_moment,
    cross_query_square,
    cross_pair_weight,
    cross_pair_moment,
    cross_pair_square,
    cross_out_weight,
    cross_out_moment,
    cross_out_square,
    gate_up_weight,
    gate_up_moment,
    gate_up_square,
    down_weight,
    down_moment,
    down_square,
):
    seqs, cap, width = tokens.shape
    cond_len = conditioning.shape[1]
    pieces = piece_lengths.shape[1]
    scale = HD ** (-0.5)
    shards = lax.axis_size("shard")
    ctxs = lax.axis_size("ctx")
    ctx_index = lax.axis_index("ctx")
    tp_index = lax.axis_index("tp")
    owned = qkv_weight.shape[0]
    local_width = qkv_weight.shape[2]
    units_half = down_weight.shape[1]
    few = local_width // ctxs
    heads_few = few // HD
    wide = -(-few // LANES) * LANES
    units = units_half // shards

    latent_order = (tp_index + jnp.arange(seqs, dtype=jnp.int32)) % seqs
    piece_order = (ctx_index + jnp.arange(pieces, dtype=jnp.int32)) % pieces
    mine = lambda array: lax.dynamic_index_in_dim(array, latent_order[0], 0, keepdims=False)
    others = lambda array: lax.dynamic_index_in_dim(array, latent_order[1], 0, keepdims=False)

    def both(array):
        return jnp.stack([mine(array), others(array)])

    offsets = jnp.cumsum(piece_lengths, axis=1) - piece_lengths
    slot = jnp.arange(cap, dtype=jnp.int32)
    lengths_here = both(piece_lengths)[:, piece_order]
    offsets_here = both(offsets)[:, piece_order]
    starts_here = both(start_positions)
    positions = (starts_here[:, None, None] + offsets_here[:, :, None] + slot).reshape(-1)
    key_valid = (slot < lengths_here[:, :, None]).reshape(-1)
    key_mask = jnp.broadcast_to(key_valid.astype(fl)[:, None], (key_valid.shape[0], LANES))
    tables = rotary_tables(positions)
    own_valid = (slot < lengths_here[0, 0]).astype(fl)[:, None]

    tokens_mine = mine(tokens)
    tokens_other = others(tokens)
    token_blocks = ring_gather(tokens_mine)
    token_swapped = [tokens_other] + [swap(block) for block in token_blocks[1:]]
    tokens_all = jnp.concatenate(token_blocks + token_swapped, axis=0)
    dy_mine = mine(cotangent).astype(fl) * own_valid
    dy_low = dy_mine.astype(bf)
    dy_blocks = square_gather(dy_low)
    dy_all = jnp.concatenate([b for block in dy_blocks for b in (block, swap(block))], axis=0)

    kinds = jnp.concatenate(
        [
            qkv_weight.astype(bf),
            output_weight.astype(bf)[:, None],
            cross_pair_weight.astype(bf),
        ],
        axis=1,
    )
    n_kinds = kinds.shape[1]
    kinds = jnp.transpose(kinds.reshape(owned, n_kinds, ctxs, few), (2, 0, 1, 3)).reshape(
        ctxs, owned, n_kinds * few
    )
    gain_lanes = jnp.pad(jnp.transpose(norm_gains).astype(bf), ((0, 0), (0, LANES - 3)))
    sent_attn = jnp.concatenate(
        [kinds, jnp.broadcast_to(gain_lanes[None], (ctxs, owned, LANES))], axis=2
    )
    sent_attn = lax.all_to_all(sent_attn, "ctx", 0, 0, tiled=True)
    attn_full = lax.all_gather(
        sent_attn.reshape(ctxs * owned, -1), "shard", axis=0, tiled=True
    )
    weight_of = lambda kind: attn_full[:, kind * few : (kind + 1) * few]
    padded = lambda array: jnp.pad(array, ((0, 0), (0, wide - few)))
    qkv_wide = jnp.concatenate([padded(weight_of(kind)) for kind in range(3)], axis=1)
    output_wide = padded(weight_of(3))
    pair_full = attn_full[:, 4 * few : 6 * few]
    gains = jnp.transpose(attn_full[:, n_kinds * few : n_kinds * few + 3].astype(fl))

    cross_full = lax.all_gather(
        jnp.concatenate([cross_query_weight.astype(bf), cross_out_weight.astype(bf)], axis=1),
        ("shard", "ctx"),
        axis=0,
        tiled=True,
    )
    query_full = cross_full[:, :local_width]
    cross_out_full = cross_full[:, local_width:]

    sent_mlp = jnp.concatenate(
        [gate_up_weight.astype(bf), down_weight.astype(bf)[:, None]], axis=1
    )
    sent_mlp = jnp.transpose(sent_mlp.reshape(owned, 3, shards, units), (2, 0, 1, 3)).reshape(
        shards, owned, 3 * units
    )
    sent_mlp = lax.all_to_all(sent_mlp, "shard", 0, 0, tiled=True)
    mlp_full = lax.all_gather(sent_mlp, "ctx", axis=0, tiled=False)
    mlp_full = jnp.transpose(mlp_full, (1, 0, 2, 3)).reshape(width, 3 * units)

    total = pieces * cap
    block = total // 3
    input1, qkv = project(tokens_all, gains[0:1], qkv_wide, tables, scale, block)
    mixed_low, lse = attend(qkv, key_mask, seqs, heads_few, block)
    partial = matmul_t(mixed_low, output_wide).astype(bf).reshape(seqs, pieces, cap, width)
    from_other = swap(partial[1])
    mine_parts = [partial[0, r] + from_other[r] for r in range(pieces)]
    x_rows = tokens_mine.astype(fl)
    x_first = x_rows + ring_scatter(mine_parts)

    plain2, inverse2 = norm_parts(x_first)
    input2_mine = (plain2 * gains[1]).astype(bf)
    input2 = jnp.concatenate([input2_mine, swap(input2_mine)], axis=0)
    cross_queries = matmul(input2, query_full).astype(bf).reshape(seqs, cap, local_width)
    cond_up = -(-cond_len // 16) * 16
    cond_rows = jnp.pad(both(conditioning), ((0, 0), (0, cond_up - cond_len), (0, 0))).reshape(
        seqs * cond_up, width
    )
    own_pairs = matmul(cond_rows, pair_full).astype(bf)
    pairs = lax.all_gather(own_pairs, "ctx", axis=0, tiled=False)
    pairs = jnp.transpose(
        pairs.reshape(ctxs, seqs, cond_up, 2, few), (1, 2, 3, 0, 4)
    ).reshape(seqs, cond_up, 2 * local_width)
    cond_valid = jnp.arange(cond_up, dtype=jnp.int32)[None, :] < both(cond_counts)[:, None]
    cond_mask = jnp.broadcast_to(cond_valid.astype(fl)[:, :, None], (seqs, cond_up, LANES))
    cross_low, cross_lse = cross(cross_queries, pairs, cond_mask, scale)
    cross_low_rows = cross_low.reshape(seqs * cap, local_width)
    cross_partial = matmul_t(cross_low_rows, cross_out_full).astype(bf)
    x_second = x_first + (
        cross_partial[:cap].astype(fl) + swap(cross_partial[cap:]).astype(fl)
    )

    plain3, inverse3 = norm_parts(x_second)
    input3 = (plain3 * gains[2]).astype(bf)
    input3_all = jnp.concatenate(
        [b for block in square_gather(input3) for b in (block, swap(block))], axis=0
    )
    hidden, grad_gated, down_partial, back_partial = mlp(
        input3_all, dy_all, mlp_full, (shards * seqs * cap) // (6 * shards // 4)
    )

    def scatter_rows(partial_rows):
        parts = partial_rows.reshape(shards, seqs, cap, width)
        from_other = swap(parts[:, 1])
        return square_scatter([parts[r, 0] + from_other[r] for r in range(shards)])

    back3, grad_gain3 = norm_back(scatter_rows(back_partial), plain3, inverse3, gains[2])
    block_mine = (x_second + scatter_rows(down_partial)).astype(bf)
    block_other = swap(block_mine)

    def natural(first, second):
        straight = tp_index == 0
        return jnp.stack(
            [jnp.where(straight, first, second), jnp.where(straight, second, first)]
        )

    block_out = natural(block_mine, block_other)
    grad_gate_up = contract_rows(input3_all, grad_gated).astype(bf)
    grad_down = contract_rows(dy_all, hidden).astype(bf)
    grad_mlp = jnp.concatenate([grad_gate_up, grad_down], axis=1)
    grad_mlp = jnp.transpose(
        grad_mlp.reshape(shards, ctxs, owned, 3 * units), (1, 0, 2, 3)
    ).reshape(ctxs * shards * owned, 3 * units)
    own_mlp = lax.psum_scatter(grad_mlp, "ctx", scatter_dimension=0, tiled=True)
    own_mlp = lax.all_to_all(
        own_mlp.reshape(shards, owned, 3 * units), "shard", 0, 0, tiled=True
    )
    own_mlp = jnp.transpose(own_mlp.reshape(shards, owned, 3, units), (1, 2, 0, 3)).reshape(
        owned, 3, units_half
    )

    grad_second = dy_mine + back3
    grad2_mine = grad_second.astype(bf)
    grad2_low = jnp.concatenate([grad2_mine, swap(grad2_mine)], axis=0)
    grad_cross_out = contract_rows(grad2_low, cross_low_rows)
    grad_cmixed = matmul(grad2_low, cross_out_full).astype(bf).reshape(seqs, cap, local_width)
    grad_cq, grad_pairs = cross_back(
        cross_queries, pairs, grad_cmixed, cross_low, cross_lse, cond_mask, scale
    )
    grad_cq = grad_cq.reshape(seqs * cap, local_width)
    grad_query = contract_rows(input2, grad_cq)
    query_partial = matmul_t(grad_cq, query_full).astype(bf)
    back2, grad_gain2 = norm_back(
        query_partial[:cap].astype(fl) + swap(query_partial[cap:]).astype(fl),
        plain2,
        inverse2,
        gains[1],
    )
    own_cross = lax.psum_scatter(
        jnp.concatenate([grad_query.astype(bf), grad_cross_out.astype(bf)], axis=1),
        ("shard", "ctx"),
        scatter_dimension=0,
        tiled=True,
    ).astype(fl)
    grad_pairs = jnp.transpose(
        grad_pairs.reshape(seqs, cond_up, 2, ctxs, few), (3, 0, 1, 2, 4)
    ).reshape(ctxs * seqs * cond_up, 2 * few)
    own_pair_grads = lax.psum_scatter(grad_pairs, "ctx", scatter_dimension=0, tiled=True)
    grad_pair = contract_rows(cond_rows, own_pair_grads)

    grad_first = grad_second + back2
    grad1_mine = grad_first.astype(bf)
    grad1_blocks = ring_gather(grad1_mine)
    grad1_low = jnp.concatenate(
        grad1_blocks + [swap(block) for block in grad1_blocks], axis=0
    )
    grad_output = contract_rows(grad1_low, mixed_low)
    grad_mixed = matmul(grad1_low, output_wide).astype(bf)
    grad_projected = attend_back(
        qkv, grad_mixed, mixed_low, lse, key_mask, tables, seqs, heads_few, block, scale
    )
    first_partial = matmul_t(grad_projected, qkv_wide).astype(bf).reshape(
        seqs, pieces, cap, width
    )
    from_other = swap(first_partial[1])
    first_parts = [first_partial[0, r] + from_other[r] for r in range(pieces)]
    plain1, inverse1 = norm_parts(x_rows)
    back1, grad_gain1 = norm_back(ring_scatter(first_parts), plain1, inverse1, gains[0])
    tokens_grad_mine = grad_first + back1
    tokens_grad = natural(tokens_grad_mine, swap(tokens_grad_mine))
    grad_qkv = contract_rows(input1, grad_projected)

    gain_grads = jnp.pad(
        jnp.stack([grad_gain1, grad_gain2, grad_gain3], axis=1), ((0, 0), (0, LANES - 3))
    )
    grad_attn = jnp.concatenate(
        [grad_qkv[:, kind * wide : kind * wide + few].astype(bf) for kind in range(3)]
        + [grad_output[:, :few].astype(bf), grad_pair.astype(bf), gain_grads.astype(bf)],
        axis=1,
    )
    own_attn = lax.psum_scatter(grad_attn, "shard", scatter_dimension=0, tiled=True)
    own_attn = lax.all_to_all(own_attn.reshape(ctxs, owned, -1), "ctx", 0, 0, tiled=True)
    own_gains = jnp.sum(own_attn[:, :, n_kinds * few : n_kinds * few + 3].astype(fl), axis=0)
    own_gains = jnp.transpose(own_gains + swap(own_gains))
    own_kinds = jnp.transpose(
        own_attn[:, :, : n_kinds * few].reshape(ctxs, owned, n_kinds, few), (1, 2, 0, 3)
    ).reshape(owned, n_kinds, local_width).astype(fl)
    own_qkv = own_kinds[:, :3]
    own_output = own_kinds[:, 3]
    own_pair = own_kinds[:, 4:]
    own_query = own_cross[:, :local_width]
    own_cross_out = own_cross[:, local_width:]
    own_gate_up = own_mlp[:, :2].astype(fl)
    own_down = own_mlp[:, 2].astype(fl)

    squares = jnp.sum(own_kinds * own_kinds) + jnp.sum(own_cross * own_cross)
    squares = squares + jnp.sum(own_gate_up * own_gate_up) + jnp.sum(own_down * own_down)
    squares = squares + jnp.sum(own_gains * own_gains) / float(lax.axis_size("tp"))
    total_square = total_over_all(jnp.broadcast_to(squares, (8, LANES)))[0, 0]
    grad_norm = jnp.sqrt(total_square)
    clip_scale = clip_norm / jnp.maximum(grad_norm, clip_norm)

    def step(weight, moment, square, grad):
        return adam_step(weight, moment, square, grad, clip_scale, weight_decay, learn_rate)

    return (
        block_out,
        tokens_grad,
        grad_norm,
        *adam_step(
            norm_gains, gains_moment, gains_square, own_gains, clip_scale, 0.0, gain_rate
        ),
        *step(qkv_weight, qkv_moment, qkv_square, own_qkv),
        *step(output_weight, output_moment, output_square, own_output),
        *step(cross_query_weight, cross_query_moment, cross_query_square, own_query),
        *step(cross_pair_weight, cross_pair_moment, cross_pair_square, own_pair),
        *step(cross_out_weight, cross_out_moment, cross_out_square, own_cross_out),
        *step(gate_up_weight, gate_up_moment, gate_up_square, own_gate_up),
        *step(down_weight, down_moment, down_square, own_down),
    )


def solution(mesh):
    in_specs = (
        P("shard", "ctx", None),
        P("shard", None, None),
        P("shard", "ctx", None),
        P("shard", None),
        P("shard"),
        P("shard"),
        P(None, ("shard", "ctx")),
        P(None, ("shard", "ctx")),
        P(None, ("shard", "ctx")),
        P(("shard", "ctx"), None, "tp"),
        P(("shard", "ctx"), None, "tp"),
        P(("shard", "ctx"), None, "tp"),
        P(("shard", "ctx"), "tp"),
        P(("shard", "ctx"), "tp"),
        P(("shard", "ctx"), "tp"),
        P(("shard", "ctx"), "tp"),
        P(("shard", "ctx"), "tp"),
        P(("shard", "ctx"), "tp"),
        P(("shard", "ctx"), None, "tp"),
        P(("shard", "ctx"), None, "tp"),
        P(("shard", "ctx"), None, "tp"),
        P(("shard", "ctx"), "tp"),
        P(("shard", "ctx"), "tp"),
        P(("shard", "ctx"), "tp"),
        P(("shard", "ctx"), None, "tp"),
        P(("shard", "ctx"), None, "tp"),
        P(("shard", "ctx"), None, "tp"),
        P(("shard", "ctx"), "tp"),
        P(("shard", "ctx"), "tp"),
        P(("shard", "ctx"), "tp"),
    )
    out_specs = (
        P("shard", "ctx", None),
        P("shard", "ctx", None),
        P(),
        P(None, ("shard", "ctx")),
        P(None, ("shard", "ctx")),
        P(None, ("shard", "ctx")),
        P(("shard", "ctx"), None, "tp"),
        P(("shard", "ctx"), None, "tp"),
        P(("shard", "ctx"), None, "tp"),
        P(("shard", "ctx"), "tp"),
        P(("shard", "ctx"), "tp"),
        P(("shard", "ctx"), "tp"),
        P(("shard", "ctx"), "tp"),
        P(("shard", "ctx"), "tp"),
        P(("shard", "ctx"), "tp"),
        P(("shard", "ctx"), None, "tp"),
        P(("shard", "ctx"), None, "tp"),
        P(("shard", "ctx"), None, "tp"),
        P(("shard", "ctx"), "tp"),
        P(("shard", "ctx"), "tp"),
        P(("shard", "ctx"), "tp"),
        P(("shard", "ctx"), None, "tp"),
        P(("shard", "ctx"), None, "tp"),
        P(("shard", "ctx"), None, "tp"),
        P(("shard", "ctx"), "tp"),
        P(("shard", "ctx"), "tp"),
        P(("shard", "ctx"), "tp"),
    )
    return jax.shard_map(local, mesh=mesh, in_specs=in_specs, out_specs=out_specs, check_vma=False)
```

```python
import functools

import jax
import jax.numpy as jnp
from jax import lax
from jax.experimental import pallas as pl
from jax.experimental.pallas import tpu as pltpu
from jax.sharding import PartitionSpec as P

HD = 64
ROT = 32
STEP = 7
LANES = 128
MOST_BLOCKS = 8


norm_eps = 1e-05
clip_norm = 1.0
beta_first = 0.9
beta_second = 0.999
learn_rate = 0.03
gain_rate = 0.75
weight_decay = 0.01
adam_eps = 1e-08
masked_score = -1e30
bf = jnp.bfloat16
fl = jnp.float32
MIB = 1024 * 1024


def params(mib):
    return pltpu.CompilerParams(vmem_limit_bytes=mib * MIB)


def whole(shape):
    return pl.BlockSpec(shape, lambda *index: (0,) * len(shape))


def matmul_t(left, right):
    return lax.dot_general(
        left, right, (((1,), (1,)), ((), ())), preferred_element_type=jnp.float32
    )


def matmul(left, right):
    return jnp.dot(left, right, preferred_element_type=jnp.float32)


def contract_rows(left, right):
    return lax.dot_general(
        left, right, (((0,), (0,)), ((), ())), preferred_element_type=jnp.float32
    )


def flip(block):
    return block.astype(fl).T


def norm_parts(rows):
    middle = jnp.mean(rows, axis=-1, keepdims=True)
    centred = rows - middle
    variance = jnp.mean(centred * centred, axis=-1, keepdims=True)
    inverse = lax.rsqrt(variance + norm_eps)
    return (centred * inverse, inverse)


def norm_back(grad_out, plain, inverse, gain):
    scaled = grad_out * gain
    term_mean = jnp.mean(scaled, axis=-1, keepdims=True)
    term_along = jnp.mean(scaled * plain, axis=-1, keepdims=True)
    return (inverse * (scaled - term_mean - plain * term_along), jnp.sum(grad_out * plain, axis=0))


def turn(lanes, cosine, sine_up, sine_down):
    return (
        lanes * cosine
        + pltpu.roll(lanes, ROT // 2, 1) * sine_up
        + pltpu.roll(lanes, LANES - ROT // 2, 1) * sine_down
    )


def pick(step, refs, held):
    for k, ref in enumerate(refs):

        @pl.when(step == k)
        def _(ref=ref):
            held[...] = ref[...]


def one_buffer(shape):
    return pl.BlockSpec(
        shape, lambda *index: (0,) * len(shape), pipeline_mode=pl.Buffered(buffer_count=1)
    )


def stacked(shape):
    return pl.BlockSpec((1,) + shape, lambda i: (i, 0, 0))


def project_kernel(count, few, scale, *refs):
    x_refs = refs[:count]
    gain_ref, w_ref, cos_ref, up_ref, down_ref, a_ref, qkv_ref, held = refs[count:]
    pick(pl.program_id(0), x_refs, held)
    plain, _ = norm_parts(held[...].astype(fl))
    rows = (plain * gain_ref[...]).astype(bf)
    a_ref[0] = rows
    projected = matmul(rows, w_ref[:, : 3 * few])
    cosine, up, down = cos_ref[0], up_ref[0], down_ref[0]
    lane = lax.broadcasted_iota(jnp.int32, cosine.shape, 1)
    for start in range(0, 2 * few, LANES):
        turned = turn(projected[:, start : start + LANES], cosine, up, down)
        if start < few:
            turned = jnp.where(lane < few - start, turned * scale, turned)
        qkv_ref[0, :, start : start + LANES] = turned.astype(bf)
    qkv_ref[0, :, 2 * few :] = projected[:, 2 * few :].astype(bf)


def project(blocks, gain, weight, tables, scale, few):
    count = len(blocks)
    rows, width = blocks[0].shape
    used = -(-3 * few // LANES) * LANES
    return pl.pallas_call(
        functools.partial(project_kernel, count, few, scale),
        grid=(count,),
        in_specs=[one_buffer((rows, width))] * count
        + [
            whole((1, width)),
            one_buffer((width, used)),
            stacked((rows, LANES)),
            stacked((rows, LANES)),
            stacked((rows, LANES)),
        ],
        out_specs=[stacked((rows, width)), stacked((rows, 3 * few))],
        out_shape=[
            jax.ShapeDtypeStruct((count, rows, width), bf),
            jax.ShapeDtypeStruct((count, rows, 3 * few), bf),
        ],
        scratch_shapes=[pltpu.VMEM((rows, width), bf)],
        compiler_params=params(48),
        cost_estimate=pl.CostEstimate(
            flops=2 * count * rows * width * 4 * few,
            bytes_accessed=count * rows * (4 * width + 6 * few),
            transcendentals=0,
        ),
        name="project",
    )(*blocks, gain, weight, *(table.reshape(count, rows, LANES) for table in tables))


def attend_kernel(heads, wide, block, qkv_ref, mask_ref, o_ref, lse_ref):
    mask = mask_ref[:, 0:1] > 0.5
    total = qkv_ref.shape[0]
    for h in range(heads):
        low, high = h * HD, (h + 1) * HD
        keys = qkv_ref[:, wide + low : wide + high]
        values_t = flip(qkv_ref[:, 2 * wide + low : 2 * wide + high]).astype(bf)
        for b in range(total // block):
            queries = qkv_ref[b * block : (b + 1) * block, low:high]
            scores = jnp.where(mask, matmul_t(keys, queries), masked_score)
            peak = jnp.max(scores, axis=0, keepdims=True)
            weights = jnp.exp(scores - peak)
            sums = jnp.sum(weights, axis=0, keepdims=True)
            mixed = matmul(values_t, weights.astype(bf)) / sums
            o_ref[b * block : (b + 1) * block, low:high] = mixed.T.astype(bf)
            spot = h * (total // block) + b
            lse_ref[0, spot : spot + 1, :] = peak + jnp.log(sums)


def attend(qkv, mask, latents, heads, block):
    rows, lanes = qkv.shape
    wide = lanes // 3
    total = rows // latents
    spots = heads * (total // block)
    spots_up = -(-spots // 8) * 8
    return pl.pallas_call(
        functools.partial(attend_kernel, heads, wide, block),
        grid=(latents,),
        in_specs=[
            pl.BlockSpec((total, lanes), lambda i: (i, 0)),
            pl.BlockSpec((total, LANES), lambda i: (i, 0)),
        ],
        out_specs=[
            pl.BlockSpec((total, wide), lambda i: (i, 0)),
            pl.BlockSpec((1, spots_up, block), lambda i: (i, 0, 0)),
        ],
        out_shape=[
            jax.ShapeDtypeStruct((rows, wide), bf),
            jax.ShapeDtypeStruct((latents, spots_up, block), fl),
        ],
        compiler_params=params(48),
        cost_estimate=pl.CostEstimate(
            flops=latents * heads * total * total * 16 * HD,
            bytes_accessed=rows * 4 * wide * 2,
            transcendentals=latents * heads * total * total,
        ),
        name="attend",
    )(qkv, mask)


def attend_back_kernel(
    heads, wide, block, scale, qkv_ref, do_ref, o_ref, lse_ref, mask_ref, cos_ref, up_ref, down_ref,
    out_ref, work_ref,
):
    mask = mask_ref[:, 0:1] > 0.5
    total = qkv_ref.shape[0]
    ones = jnp.ones((8, HD), fl)
    for h in range(heads):
        low, high = h * HD, (h + 1) * HD
        keys = qkv_ref[:, wide + low : wide + high]
        keys_t = flip(keys).astype(bf)
        values = qkv_ref[:, 2 * wide + low : 2 * wide + high]
        grad_keys = jnp.zeros((total, HD), fl)
        grad_values = jnp.zeros((total, HD), fl)
        for b in range(total // block):
            queries = qkv_ref[b * block : (b + 1) * block, low:high]
            grads = do_ref[b * block : (b + 1) * block, low:high]
            mixed = o_ref[b * block : (b + 1) * block, low:high]
            spot = h * (total // block) + b
            scores = jnp.where(mask, matmul_t(keys, queries), masked_score)
            probs = jnp.exp(scores - lse_ref[0, spot : spot + 1, :])
            delta = lax.dot_general(
                ones,
                grads.astype(fl) * mixed.astype(fl),
                (((1,), (1,)), ((), ())),
                precision=lax.Precision.HIGHEST,
                preferred_element_type=fl,
            )[0:1]
            grad_scores = (probs * (matmul_t(values, grads) - delta)).astype(bf)
            grad_values += matmul(probs.astype(bf), grads)
            grad_keys += matmul(grad_scores, queries)
            grad_queries = matmul(keys_t, grad_scores) * scale
            work_ref[b * block : (b + 1) * block, low:high] = grad_queries.T
        work_ref[:, wide + low : wide + high] = grad_keys
        work_ref[:, 2 * wide + low : 2 * wide + high] = grad_values
    cosine, up, down = cos_ref[...], -up_ref[...], -down_ref[...]
    for start in range(0, 2 * wide, LANES):
        out_ref[:, start : start + LANES] = turn(
            work_ref[:, start : start + LANES], cosine, up, down
        ).astype(bf)
    out_ref[:, 2 * wide :] = work_ref[:, 2 * wide :].astype(bf)


def attend_back(qkv, grads, mixed, lse, mask, tables, latents, heads, block, scale):
    rows, lanes = qkv.shape
    wide = lanes // 3
    total = rows // latents
    by_latent = lambda n: pl.BlockSpec((total, n), lambda i: (i, 0))
    return pl.pallas_call(
        functools.partial(attend_back_kernel, heads, wide, block, scale),
        grid=(latents,),
        in_specs=[
            by_latent(lanes),
            by_latent(wide),
            by_latent(wide),
            pl.BlockSpec((1,) + lse.shape[1:], lambda i: (i, 0, 0)),
            by_latent(LANES),
            by_latent(LANES),
            by_latent(LANES),
            by_latent(LANES),
        ],
        out_specs=by_latent(lanes),
        out_shape=jax.ShapeDtypeStruct((rows, lanes), bf),
        scratch_shapes=[pltpu.VMEM((total, lanes), fl)],
        compiler_params=params(56),
        cost_estimate=pl.CostEstimate(
            flops=latents * heads * total * total * 40 * HD,
            bytes_accessed=rows * 10 * wide * 2,
            transcendentals=latents * heads * total * total,
        ),
        name="attend_back",
    )(qkv, grads, mixed, lse, mask, *tables)


def cross_kernel(heads, scale, q_ref, kv_ref, mask_ref, o_ref, lse_ref):
    mask = mask_ref[0, :, 0:1] > 0.5
    wide = heads * HD
    for first in range(0, heads, 2):
        pair = []
        for h in (first, first + 1):
            low, high = h * HD, (h + 1) * HD
            keys = kv_ref[0, :, low:high]
            values_t = flip(kv_ref[0, :, wide + low : wide + high]).astype(bf)
            scores = jnp.where(mask, matmul_t(keys, q_ref[0, :, low:high]) * scale, masked_score)
            peak = jnp.max(scores, axis=0, keepdims=True)
            weights = jnp.exp(scores - peak)
            sums = jnp.sum(weights, axis=0, keepdims=True)
            pair.append(matmul(values_t, weights.astype(bf)) / sums)
            lse_ref[0, h : h + 1, :] = peak + jnp.log(sums)
        o_ref[0, :, first * HD : (first + 2) * HD] = (
            jnp.concatenate(pair, axis=0).T.astype(bf)
        )


def cross(queries, pairs, mask, scale):
    latents, rows, wide = queries.shape
    heads = wide // HD
    heads_up = -(-heads // 8) * 8
    one = lambda shape: pl.BlockSpec((1,) + shape, lambda i: (i, 0, 0))
    return pl.pallas_call(
        functools.partial(cross_kernel, heads, scale),
        grid=(latents,),
        in_specs=[one((rows, wide)), one(pairs.shape[1:]), one(mask.shape[1:])],
        out_specs=[one((rows, wide)), one((heads_up, rows))],
        out_shape=[
            jax.ShapeDtypeStruct((latents, rows, wide), bf),
            jax.ShapeDtypeStruct((latents, heads_up, rows), fl),
        ],
        compiler_params=params(32),
        cost_estimate=pl.CostEstimate(
            flops=latents * heads * rows * 256 * 16 * HD,
            bytes_accessed=8 * latents * rows * wide,
            transcendentals=latents * heads * rows * 144,
        ),
        name="cross",
    )(queries, pairs, mask)


def cross_back_kernel(
    heads, scale, q_ref, kv_ref, do_ref, o_ref, lse_ref, mask_ref, dq_ref, dkv_ref
):
    mask = mask_ref[0, :, 0:1] > 0.5
    wide = heads * HD
    ones = jnp.ones((8, HD), fl)
    for first in range(0, heads, 2):
        pair = []
        grad_keys = []
        grad_values = []
        for h in (first, first + 1):
            low, high = h * HD, (h + 1) * HD
            keys = kv_ref[0, :, low:high]
            keys_t = flip(keys).astype(bf)
            values = kv_ref[0, :, wide + low : wide + high]
            queries = q_ref[0, :, low:high]
            grads = do_ref[0, :, low:high]
            scores = jnp.where(mask, matmul_t(keys, queries) * scale, masked_score)
            probs = jnp.exp(scores - lse_ref[0, h : h + 1, :])
            delta = lax.dot_general(
                ones,
                grads.astype(fl) * o_ref[0, :, low:high].astype(fl),
                (((1,), (1,)), ((), ())),
                precision=lax.Precision.HIGHEST,
                preferred_element_type=fl,
            )[0:1]
            grad_scores = (probs * (matmul_t(values, grads) - delta)).astype(bf)
            grad_values.append(matmul(probs.astype(bf), grads))
            grad_keys.append(matmul(grad_scores, queries) * scale)
            pair.append(matmul(keys_t, grad_scores) * scale)
        low, high = first * HD, (first + 2) * HD
        dq_ref[0, :, low:high] = jnp.concatenate(pair, axis=0).T.astype(bf)
        dkv_ref[0, :, low:high] = jnp.concatenate(grad_keys, axis=1).astype(bf)
        dkv_ref[0, :, wide + low : wide + high] = jnp.concatenate(grad_values, axis=1).astype(bf)


def cross_back(queries, pairs, grads, mixed, lse, mask, scale):
    latents, rows, wide = queries.shape
    heads = wide // HD
    one = lambda shape: pl.BlockSpec((1,) + shape, lambda i: (i, 0, 0))
    return pl.pallas_call(
        functools.partial(cross_back_kernel, heads, scale),
        grid=(latents,),
        in_specs=[
            one((rows, wide)),
            one(pairs.shape[1:]),
            one((rows, wide)),
            one((rows, wide)),
            one(lse.shape[1:]),
            one(mask.shape[1:]),
        ],
        out_specs=[one((rows, wide)), one(pairs.shape[1:])],
        out_shape=[
            jax.ShapeDtypeStruct(queries.shape, bf),
            jax.ShapeDtypeStruct(pairs.shape, bf),
        ],
        compiler_params=params(32),
        cost_estimate=pl.CostEstimate(
            flops=latents * heads * rows * 256 * 40 * HD,
            bytes_accessed=12 * latents * rows * wide,
            transcendentals=latents * heads * rows * 144,
        ),
        name="cross_back",
    )(queries, pairs, grads, mixed, lse, mask)


def mix_back_kernel(count, *refs):
    g_refs = refs[:count]
    w_ref, o_ref, do_ref, grad_ref, held, total = refs[count:]
    step = pl.program_id(0)
    few = o_ref.shape[2]

    @pl.when(step == 0)
    def _():
        total[...] = jnp.zeros_like(total)

    pick(step, g_refs, held)
    rows = held[...]
    do_ref[0] = matmul(rows, w_ref[:, :few]).astype(bf)
    total[...] += matmul(flip(o_ref[0]).astype(bf), rows)

    @pl.when(step == count - 1)
    def _():
        grad_ref[...] = total[...].T.astype(bf)


def mix_back(blocks, weight, mixed):
    count = len(blocks)
    rows, width = blocks[0].shape
    few = mixed.shape[2]
    return pl.pallas_call(
        functools.partial(mix_back_kernel, count),
        grid=(count,),
        in_specs=[one_buffer((rows, width))] * count
        + [one_buffer(weight.shape), stacked((rows, few))],
        out_specs=[stacked((rows, few)), whole((width, few))],
        out_shape=[
            jax.ShapeDtypeStruct((count, rows, few), bf),
            jax.ShapeDtypeStruct((width, few), bf),
        ],
        scratch_shapes=[pltpu.VMEM((rows, width), bf), pltpu.VMEM((few, width), fl)],
        compiler_params=params(48),
        cost_estimate=pl.CostEstimate(
            flops=4 * count * rows * width * 256,
            bytes_accessed=2 * count * rows * (width + 2 * few) + 8 * width * few,
            transcendentals=0,
        ),
        name="mix_back",
    )(*blocks, weight, mixed)


def mlp_kernel(count, given, *refs):
    a_refs, dy_refs = refs[:given], refs[given : 2 * given]
    (
        gate_ref,
        up_ref,
        down_ref,
        a_ref,
        dy_ref,
        h_ref,
        dgu_ref,
        out_other,
        out_own,
        da_other,
        da_own,
        weight,
        a_held,
        dy_held,
    ) = refs[2 * given :]
    step = pl.program_id(0)
    ctxs, shards, owned, units = gate_ref.shape

    @pl.when(step == 0)
    def _():
        for s in range(shards):
            for c in range(ctxs):
                row = (s * ctxs + c) * owned
                for k, kind in enumerate((gate_ref, up_ref, down_ref)):
                    weight[row : row + owned, k * units : (k + 1) * units] = kind[c, s]

    if given == count:
        pick(step, a_refs, a_held)
        pick(step, dy_refs, dy_held)
    else:
        a_held[...] = a_refs[0][0]
        dy_held[...] = dy_refs[0][0]
    rows = a_held[...]
    grads = dy_held[...]
    a_ref[0] = rows
    dy_ref[0] = grads
    gate = matmul(rows, weight[:, :units])
    upward = matmul(rows, weight[:, units : 2 * units])
    sigmoid = jax.nn.sigmoid(gate)
    activated = gate * sigmoid
    hidden = (activated * upward).astype(bf)
    h_ref[0] = hidden
    grad_hidden = matmul(grads, weight[:, 2 * units :])
    grad_gate = (grad_hidden * upward * sigmoid * (1.0 + gate * (1.0 - sigmoid))).astype(bf)
    grad_up = (grad_hidden * activated).astype(bf)
    dgu_ref[0, :, :units] = grad_gate
    dgu_ref[0, :, units:] = grad_up
    da = (
        matmul_t(grad_gate, weight[:, :units]) + matmul_t(grad_up, weight[:, units : 2 * units])
    ).astype(bf)
    out = matmul_t(hidden, weight[:, 2 * units :]).astype(bf)

    @pl.when(step < count // 2)
    def _():
        da_other[0] = da
        out_other[0] = out

    @pl.when(step >= count // 2)
    def _():
        da_own[0] = da
        out_own[0] = out


def mlp(blocks, grads, weights):
    count = len(blocks)
    half = count // 2
    rows, width = blocks[0].shape
    units = weights[0].shape[3]
    if count <= MOST_BLOCKS:
        feeds = one_buffer((rows, width))
    else:
        feeds = stacked((rows, width))
        blocks, grads = [jnp.stack(blocks)], [jnp.stack(grads)]
    given = len(blocks)
    first = pl.BlockSpec((1, rows, width), lambda i: (jnp.minimum(i, half - 1), 0, 0))
    second = pl.BlockSpec((1, rows, width), lambda i: (jnp.maximum(i - half, 0), 0, 0))
    return pl.pallas_call(
        functools.partial(mlp_kernel, count, given),
        grid=(count,),
        in_specs=[feeds] * (2 * given) + [one_buffer(weights[0].shape)] * 3,
        out_specs=[
            stacked((rows, width)),
            stacked((rows, width)),
            stacked((rows, units)),
            stacked((rows, 2 * units)),
            first,
            second,
            first,
            second,
        ],
        out_shape=[
            jax.ShapeDtypeStruct((count, rows, width), bf),
            jax.ShapeDtypeStruct((count, rows, width), bf),
            jax.ShapeDtypeStruct((count, rows, units), bf),
            jax.ShapeDtypeStruct((count, rows, 2 * units), bf),
        ]
        + [jax.ShapeDtypeStruct((half, rows, width), bf)] * 4,
        scratch_shapes=[
            pltpu.VMEM((width, 3 * units), bf),
            pltpu.VMEM((rows, width), bf),
            pltpu.VMEM((rows, width), bf),
        ],
        compiler_params=params(60),
        cost_estimate=pl.CostEstimate(
            flops=12 * count * rows * width * units,
            bytes_accessed=2 * count * rows * (6 * width + 3 * units) + 6 * width * units,
            transcendentals=count * rows * units,
        ),
        name="mlp",
    )(*blocks, *grads, *weights)


def after(value, *others):
    return lax.optimization_barrier((value,) + others)[0]


def swap(value):
    return lax.ppermute(value, "tp", [(0, 1), (1, 0)])


def ring_shift(value, by):
    size = lax.axis_size("ctx")
    return lax.ppermute(value, "ctx", [(i, (i - by) % size) for i in range(size)])


def cross_over(value, bits):
    size = lax.axis_size("shard")
    return lax.ppermute(value, "shard", [(i, i ^ bits) for i in range(size)])


def ring_gather(own, first=(), second=()):
    size = lax.axis_size("ctx")
    if size != 4:
        return [own] + [after(ring_shift(own, r), *second) for r in range(1, size)]
    half = own.shape[-1] // 2
    following = after(ring_shift(own, 1), *first)
    before = after(ring_shift(own, -1), *first)
    far = jnp.concatenate(
        [
            after(ring_shift(following[:, :half], 1), *second),
            after(ring_shift(before[:, half:], -1), *second),
        ],
        axis=-1,
    )
    return [own, following, far, before]


def ring_scatter(parts, first=(), second=()):
    if lax.axis_size("ctx") != 4:
        total = parts[0].astype(fl)
        for r in range(1, len(parts)):
            total = total + after(ring_shift(parts[r], -r), *second).astype(fl)
        return total
    half = parts[0].shape[-1] // 2
    by_after = after(ring_shift(parts[2][:, :half], -1), *first)
    by_before = after(ring_shift(parts[2][:, half:], 1), *first)
    to_after = jnp.concatenate([parts[1][:, :half] + by_after, parts[1][:, half:]], axis=-1)
    to_before = jnp.concatenate([parts[3][:, :half], parts[3][:, half:] + by_before], axis=-1)
    from_before = after(ring_shift(to_after, -1), *second)
    from_after = after(ring_shift(to_before, 1), *second)
    return parts[0].astype(fl) + from_before.astype(fl) + from_after.astype(fl)


def ring_exchange(parts):
    return [parts[0]] + [ring_shift(part, -r) for r, part in enumerate(parts[1:], 1)]


def square_exchange(parts):
    return [parts[0]] + [cross_over(part, r) for r, part in enumerate(parts[1:], 1)]


def at(array, index):
    return lax.dynamic_index_in_dim(array, index, 0, keepdims=False)


def rows_at(array, index, count):
    return lax.dynamic_slice_in_dim(array, index * count, count, 0)


def place(blocks, indices):
    out = jnp.zeros((len(blocks),) + blocks[0].shape, blocks[0].dtype)
    for block, index in zip(blocks, indices):
        out = lax.dynamic_update_index_in_dim(out, block, index, 0)
    return out


def square_gather(own, first=(), second=()):
    size = lax.axis_size("shard")
    if size != 4:
        return [own] + [after(cross_over(own, r), *second) for r in range(1, size)]
    half = own.shape[-1] // 2
    one = after(cross_over(own, 1), *first)
    two = after(cross_over(own, 2), *first)
    three = jnp.concatenate(
        [
            after(cross_over(two[:, :half], 1), *second),
            after(cross_over(one[:, half:], 2), *second),
        ],
        axis=-1,
    )
    return [own, one, two, three]


def square_scatter(parts, first=(), second=()):
    size = lax.axis_size("shard")
    if size != 4:
        total = parts[0].astype(fl)
        for r in range(1, size):
            total = total + after(cross_over(parts[r], r), *second).astype(fl)
        return total
    half = parts[0].shape[-1] // 2
    by_one = after(cross_over(parts[3][:, :half], 1), *first)
    by_two = after(cross_over(parts[3][:, half:], 2), *first)
    to_two = jnp.concatenate([parts[2][:, :half] + by_one, parts[2][:, half:]], axis=-1)
    to_one = jnp.concatenate([parts[1][:, :half], parts[1][:, half:] + by_two], axis=-1)
    from_one = after(cross_over(to_one, 1), *second)
    from_two = after(cross_over(to_two, 2), *second)
    return parts[0].astype(fl) + from_one.astype(fl) + from_two.astype(fl)


def total_over_all(value):
    for axis in ("tp", "shard", "ctx"):
        size = lax.axis_size(axis)
        bit = 1
        while bit < size:
            value = value + lax.ppermute(value, axis, [(i, i ^ bit) for i in range(size)])
            bit *= 2
    return value


def adam_step(weight, moment, square, grad, scale, decay, rate):
    grad = grad * scale
    moment_new = beta_first * moment + (1.0 - beta_first) * grad
    square_new = beta_second * square + (1.0 - beta_second) * grad * grad
    moment_hat = moment_new / (1.0 - beta_first**STEP)
    square_hat = square_new / (1.0 - beta_second**STEP)
    weight_new = weight - rate * (moment_hat / (jnp.sqrt(square_hat) + adam_eps) + decay * weight)
    return (moment_new, square_new, weight_new)


def rotary_tables(positions):
    lane = jnp.arange(LANES, dtype=jnp.int32) % HD
    step = (lane % (ROT // 2)).astype(fl) * 2.0 / ROT
    frequency = jnp.where(lane < ROT, 10000.0 ** (-step), 0.0)
    angles = positions.astype(fl)[:, None] * frequency[None, :]
    sine = jnp.sin(angles)
    up = jnp.where((lane >= ROT // 2) & (lane < ROT), sine, 0.0)
    down = jnp.where(lane < ROT // 2, -sine, 0.0)
    return (jnp.cos(angles), up, down)


def local(
    tokens,
    conditioning,
    cotangent,
    piece_lengths,
    start_positions,
    cond_counts,
    norm_gains,
    gains_moment,
    gains_square,
    qkv_weight,
    qkv_moment,
    qkv_square,
    output_weight,
    output_moment,
    output_square,
    cross_query_weight,
    cross_query_moment,
    cross_query_square,
    cross_pair_weight,
    cross_pair_moment,
    cross_pair_square,
    cross_out_weight,
    cross_out_moment,
    cross_out_square,
    gate_up_weight,
    gate_up_moment,
    gate_up_square,
    down_weight,
    down_moment,
    down_square,
):
    seqs, cap, width = tokens.shape
    cond_len = conditioning.shape[1]
    pieces = piece_lengths.shape[1]
    scale = HD ** (-0.5)
    shards = lax.axis_size("shard")
    ctxs = lax.axis_size("ctx")
    shard_index = lax.axis_index("shard")
    ctx_index = lax.axis_index("ctx")
    tp_index = lax.axis_index("tp")
    owned = qkv_weight.shape[0]
    local_width = qkv_weight.shape[2]
    units_half = down_weight.shape[1]
    few = local_width // ctxs
    heads_few = few // HD
    units = units_half // shards

    latent_order = (tp_index + jnp.arange(seqs, dtype=jnp.int32)) % seqs
    piece_order = (ctx_index + jnp.arange(pieces, dtype=jnp.int32)) % pieces
    mine = lambda array: lax.dynamic_index_in_dim(array, latent_order[0], 0, keepdims=False)
    others = lambda array: lax.dynamic_index_in_dim(array, latent_order[1], 0, keepdims=False)

    def both(array):
        return jnp.stack([mine(array), others(array)])

    offsets = jnp.cumsum(piece_lengths, axis=1) - piece_lengths
    slot = jnp.arange(cap, dtype=jnp.int32)
    lengths_here = both(piece_lengths)[:, piece_order]
    offsets_here = both(offsets)[:, piece_order]
    starts_here = both(start_positions)
    positions = (starts_here[:, None, None] + offsets_here[:, :, None] + slot).reshape(-1)
    key_valid = (slot < lengths_here[:, :, None]).reshape(-1)
    key_mask = jnp.broadcast_to(key_valid.astype(fl)[:, None], (key_valid.shape[0], LANES))
    tables = lax.optimization_barrier(rotary_tables(positions))
    own_valid = (slot < lengths_here[0, 0]).astype(fl)[:, None]

    tokens_mine = mine(tokens)
    tokens_other = others(tokens)
    dy_mine = mine(cotangent).astype(fl) * own_valid
    dy_low = dy_mine.astype(bf)

    kinds = jnp.concatenate(
        [
            qkv_weight.astype(bf),
            output_weight.astype(bf)[:, None],
            cross_pair_weight.astype(bf),
        ],
        axis=1,
    )
    n_kinds = kinds.shape[1]
    kinds = jnp.transpose(kinds.reshape(owned, n_kinds, ctxs, few), (2, 0, 1, 3)).reshape(
        ctxs, owned, n_kinds * few
    )
    gain_lanes = jnp.pad(jnp.transpose(norm_gains).astype(bf), ((0, 0), (0, LANES - 3)))
    sent_attn = jnp.concatenate(
        [kinds, jnp.broadcast_to(gain_lanes[None], (ctxs, owned, LANES))], axis=2
    )
    sent_attn = after(sent_attn, tokens_mine)
    ctx_after = [(ctx_index + r) % ctxs for r in range(ctxs)]
    ctx_before = [(ctx_index - r) % ctxs for r in range(ctxs)]
    shard_near = [shard_index ^ r for r in range(shards)]
    attn_rows = place(
        ring_exchange([at(sent_attn, index) for index in ctx_after]), ctx_before
    ).reshape(ctxs * owned, -1)
    attn_full = lax.all_gather(attn_rows, "shard", axis=0, tiled=True)
    pair_full = attn_full[:, 4 * few : 6 * few]
    output_full = attn_full[:, 3 * few : 4 * few]
    gains = jnp.transpose(attn_full[:, n_kinds * few : n_kinds * few + 3].astype(fl))

    sent_mlp = jnp.concatenate(
        [gate_up_weight.astype(bf), down_weight.astype(bf)[:, None]], axis=1
    )
    sent_mlp = jnp.transpose(sent_mlp.reshape(owned, 3, shards, units), (2, 0, 1, 3)).reshape(
        shards, owned, 3 * units
    )
    sent_mlp = place(
        square_exchange([at(sent_mlp, index) for index in shard_near]), shard_near
    )
    token_blocks = ring_gather(tokens_mine)
    sent_mlp = after(sent_mlp, token_blocks[2], attn_rows)
    over_ctx = lambda array: lax.all_gather(array, "ctx", axis=0, tiled=False)
    gate_full = over_ctx(sent_mlp[:, :, :units])
    up_full = over_ctx(sent_mlp[:, :, units : 2 * units])

    token_swapped = [tokens_other] + [swap(block) for block in token_blocks[1:]]
    token_last = after(token_swapped[-1], sent_mlp)

    total = pieces * cap
    block = total // 3
    sent_cross = jnp.concatenate(
        [cross_query_weight.astype(bf), cross_out_weight.astype(bf)], axis=1
    )
    sent_cross = after(sent_cross, token_blocks[2])
    input1, qkv = project(
        token_blocks + token_swapped[:-1] + [token_last], gains[0:1], attn_full, tables, scale, few
    )
    qkv = qkv.reshape(seqs * total, 3 * few)
    cond_up = -(-cond_len // 16) * 16
    cond_rows = jnp.pad(both(conditioning), ((0, 0), (0, cond_up - cond_len), (0, 0))).reshape(
        seqs * cond_up, width
    )
    own_pairs = after(matmul(cond_rows, pair_full).astype(bf), qkv)
    mixed_low, lse = attend(qkv, key_mask, seqs, heads_few, block)
    cross_blocks = ring_gather(sent_cross, (qkv,), (mixed_low,))
    partial = matmul_t(mixed_low, output_full).astype(bf).reshape(seqs, pieces, cap, width)
    from_other = swap(partial[1])
    mine_parts = [partial[0, r] + from_other[r] for r in range(pieces)]
    pairs = place(
        [own_pairs]
        + [after(ring_shift(own_pairs, r), mine_parts[0]) for r in range(1, ctxs)],
        ctx_after,
    )
    pairs = jnp.transpose(
        pairs.reshape(ctxs, seqs, cond_up, 2, few), (1, 2, 3, 0, 4)
    ).reshape(seqs, cond_up, 2 * local_width)
    cross_rows = place(cross_blocks, ctx_after).reshape(ctxs * owned, -1)
    cross_full = place(square_gather(cross_rows, (mine_parts[0],)), shard_near).reshape(width, -1)
    query_full = cross_full[:, :local_width]
    cross_out_full = cross_full[:, local_width:]
    x_rows = tokens_mine.astype(fl)
    x_first = x_rows + ring_scatter(mine_parts, (), (pairs, cross_full))
    dy_low = after(dy_low, cross_full)
    dy_blocks = square_gather(dy_low, (x_first,), (x_first,))
    dy_swapped = [swap(block_of) for block_of in dy_blocks]
    down_full = over_ctx(after(sent_mlp[:, :, 2 * units :], x_first))

    plain2, inverse2 = norm_parts(x_first)
    input2_mine = (plain2 * gains[1]).astype(bf)
    input2 = jnp.concatenate([input2_mine, swap(input2_mine)], axis=0)
    cross_queries = matmul(input2, query_full).astype(bf).reshape(seqs, cap, local_width)
    cond_valid = jnp.arange(cond_up, dtype=jnp.int32)[None, :] < both(cond_counts)[:, None]
    cond_mask = jnp.broadcast_to(cond_valid.astype(fl)[:, :, None], (seqs, cond_up, LANES))
    cross_low, cross_lse = cross(cross_queries, pairs, cond_mask, scale)
    cross_low_rows = cross_low.reshape(seqs * cap, local_width)
    cross_partial = matmul_t(cross_low_rows, cross_out_full).astype(bf)
    x_second = x_first + (
        cross_partial[:cap].astype(fl) + swap(cross_partial[cap:]).astype(fl)
    )

    plain3, inverse3 = norm_parts(x_second)
    input3 = (plain3 * gains[2]).astype(bf)
    input3_blocks = square_gather(input3)
    (
        input3_all,
        dy_all,
        hidden,
        grad_gated,
        down_other,
        down_own,
        back_other,
        back_own,
    ) = mlp(
        [swap(block_of) for block_of in input3_blocks] + input3_blocks,
        dy_swapped + dy_blocks,
        (gate_full, up_full, down_full),
    )
    merged = lambda array: array.reshape(-1, array.shape[-1])
    grad_down = contract_rows(merged(dy_all), merged(hidden)).astype(bf)
    grad_gate = contract_rows(merged(input3_all), merged(grad_gated)[:, :units]).astype(bf)
    grad_up = contract_rows(merged(input3_all), merged(grad_gated)[:, units:]).astype(bf)

    def add_cores(own, other):
        from_other = swap(other)
        return [own[r] + from_other[r] for r in range(own.shape[0])]

    back_sum = square_scatter(
        add_cores(back_own, back_other), (grad_down,), (grad_gate, grad_up)
    )
    back3, grad_gain3 = norm_back(back_sum, plain3, inverse3, gains[2])

    def natural(first, second):
        straight = tp_index == 0
        return jnp.stack(
            [jnp.where(straight, first, second), jnp.where(straight, second, first)]
        )

    def sum_over_ctx(array):
        by_owner = jnp.transpose(
            array.reshape(shards, ctxs, owned, array.shape[1]), (1, 0, 2, 3)
        ).reshape(ctxs * shards * owned, -1)
        return lax.psum_scatter(by_owner, "ctx", scatter_dimension=0, tiled=True)

    sum_down = sum_over_ctx(grad_down)
    sum_gate = sum_over_ctx(grad_gate)

    grad_second = dy_mine + back3
    grad2_mine = grad_second.astype(bf)
    grad2_low = jnp.concatenate([grad2_mine, swap(grad2_mine)], axis=0)
    grad_cross_out = contract_rows(grad2_low, cross_low_rows)
    grad_cmixed = matmul(grad2_low, cross_out_full).astype(bf).reshape(seqs, cap, local_width)
    grad_cq, grad_pairs = cross_back(
        cross_queries, pairs, grad_cmixed, cross_low, cross_lse, cond_mask, scale
    )
    grad_cq = grad_cq.reshape(seqs * cap, local_width)
    grad_query = contract_rows(input2, grad_cq)
    query_partial = matmul_t(grad_cq, query_full).astype(bf)
    back2, grad_gain2 = norm_back(
        query_partial[:cap].astype(fl) + swap(query_partial[cap:]).astype(fl),
        plain2,
        inverse2,
        gains[1],
    )
    grad_cross = jnp.concatenate([grad_query.astype(bf), grad_cross_out.astype(bf)], axis=1)
    grad_pairs = jnp.transpose(
        grad_pairs.reshape(seqs, cond_up, 2, ctxs, few), (3, 0, 1, 2, 4)
    ).reshape(ctxs, seqs * cond_up, 2 * few)

    grad_first = grad_second + back2
    grad1_mine = grad_first.astype(bf)
    grad1_blocks = ring_gather(grad1_mine)
    grad_cross = after(grad_cross, grad1_mine)
    cross_sum = square_scatter(
        [rows_at(grad_cross, index, ctxs * owned) for index in shard_near]
    ).astype(bf)
    grad_mixed, grad_output = mix_back(
        grad1_blocks + [swap(block_of) for block_of in grad1_blocks],
        output_full,
        mixed_low.reshape(seqs * pieces, cap, few),
    )
    sum_up = sum_over_ctx(after(grad_up, grad1_blocks[2]))
    grad_projected = attend_back(
        qkv,
        grad_mixed.reshape(seqs * total, few),
        mixed_low,
        lse,
        key_mask,
        tables,
        seqs,
        heads_few,
        block,
        scale,
    )
    first_partial = matmul_t(grad_projected, attn_full[:, : 3 * few]).astype(bf).reshape(
        seqs, pieces, cap, width
    )
    first_parts = add_cores(first_partial[0], first_partial[1])
    grad_qkv = contract_rows(merged(input1), grad_projected).astype(bf)
    grad_pairs = after(grad_pairs, grad_mixed)
    own_pair_grads = ring_scatter(
        [at(grad_pairs, index) for index in ctx_after], (grad_projected,), (first_parts[0],)
    ).astype(bf)
    grad_pair = contract_rows(cond_rows, own_pair_grads).astype(bf)
    down_own, down_other = after(down_own, grad_mixed), after(down_other, grad_mixed)
    down_parts = add_cores(down_own, after(down_other, grad_mixed))
    down_sum = square_scatter(down_parts, (first_parts[0],), (grad_qkv,))
    grad_attn = jnp.concatenate([grad_qkv, grad_output, grad_pair], axis=1)
    attn_sum = square_scatter(
        [rows_at(grad_attn, index, ctxs * owned) for index in shard_near]
    ).astype(bf)
    back1_sum = ring_scatter(first_parts, (grad_qkv,), (cross_sum, attn_sum, down_sum))
    block_mine = (x_second + down_sum).astype(bf)
    block_out = natural(block_mine, swap(block_mine))
    plain1, inverse1 = norm_parts(x_rows)
    back1, grad_gain1 = norm_back(back1_sum, plain1, inverse1, gains[0])
    tokens_grad_mine = grad_first + back1
    tokens_grad = natural(tokens_grad_mine, swap(tokens_grad_mine))

    own_cross = ring_scatter([rows_at(cross_sum, index, owned) for index in ctx_after])
    own_kinds = place(
        ring_exchange([rows_at(attn_sum, index, owned) for index in ctx_after]), ctx_before
    )
    own_kinds = jnp.transpose(
        own_kinds.reshape(ctxs, owned, n_kinds, few), (1, 2, 0, 3)
    ).reshape(owned, n_kinds, local_width).astype(fl)
    own_qkv = own_kinds[:, :3]
    own_output = own_kinds[:, 3]
    own_pair = own_kinds[:, 4:]
    own_query = own_cross[:, :local_width]
    own_cross_out = own_cross[:, local_width:]
    own_mlp = jnp.concatenate([sum_gate, sum_up, sum_down], axis=1)
    own_mlp = place(
        square_exchange([rows_at(own_mlp, index, owned) for index in shard_near]), shard_near
    )
    own_mlp = jnp.transpose(own_mlp.reshape(shards, owned, 3, units), (1, 2, 0, 3)).reshape(
        owned, 3, units_half
    )
    own_gate_up = own_mlp[:, :2].astype(fl)
    own_down = own_mlp[:, 2].astype(fl)

    squares = jnp.sum(own_kinds * own_kinds) + jnp.sum(own_cross * own_cross)
    squares = squares + jnp.sum(own_gate_up * own_gate_up) + jnp.sum(own_down * own_down)
    totals = total_over_all(
        jnp.concatenate(
            [
                jnp.stack([grad_gain1, grad_gain2, grad_gain3]),
                jnp.broadcast_to(squares, (5, width)),
            ]
        )
    )
    gain_grads = totals[:3]
    own_gains = lax.dynamic_slice_in_dim(
        gain_grads, (shard_index * ctxs + ctx_index) * owned, owned, 1
    )
    grad_norm = jnp.sqrt(totals[3, 0] + jnp.sum(gain_grads * gain_grads))
    clip_scale = clip_norm / jnp.maximum(grad_norm, clip_norm)

    def step(weight, moment, square, grad):
        return adam_step(weight, moment, square, grad, clip_scale, weight_decay, learn_rate)

    return (
        block_out,
        tokens_grad,
        grad_norm,
        *adam_step(
            norm_gains, gains_moment, gains_square, own_gains, clip_scale, 0.0, gain_rate
        ),
        *step(qkv_weight, qkv_moment, qkv_square, own_qkv),
        *step(output_weight, output_moment, output_square, own_output),
        *step(cross_query_weight, cross_query_moment, cross_query_square, own_query),
        *step(cross_pair_weight, cross_pair_moment, cross_pair_square, own_pair),
        *step(cross_out_weight, cross_out_moment, cross_out_square, own_cross_out),
        *step(gate_up_weight, gate_up_moment, gate_up_square, own_gate_up),
        *step(down_weight, down_moment, down_square, own_down),
    )


def solution(mesh):
    in_specs = (
        P("shard", "ctx", None),
        P("shard", None, None),
        P("shard", "ctx", None),
        P("shard", None),
        P("shard"),
        P("shard"),
        P(None, ("shard", "ctx")),
        P(None, ("shard", "ctx")),
        P(None, ("shard", "ctx")),
        P(("shard", "ctx"), None, "tp"),
        P(("shard", "ctx"), None, "tp"),
        P(("shard", "ctx"), None, "tp"),
        P(("shard", "ctx"), "tp"),
        P(("shard", "ctx"), "tp"),
        P(("shard", "ctx"), "tp"),
        P(("shard", "ctx"), "tp"),
        P(("shard", "ctx"), "tp"),
        P(("shard", "ctx"), "tp"),
        P(("shard", "ctx"), None, "tp"),
        P(("shard", "ctx"), None, "tp"),
        P(("shard", "ctx"), None, "tp"),
        P(("shard", "ctx"), "tp"),
        P(("shard", "ctx"), "tp"),
        P(("shard", "ctx"), "tp"),
        P(("shard", "ctx"), None, "tp"),
        P(("shard", "ctx"), None, "tp"),
        P(("shard", "ctx"), None, "tp"),
        P(("shard", "ctx"), "tp"),
        P(("shard", "ctx"), "tp"),
        P(("shard", "ctx"), "tp"),
    )
    out_specs = (
        P("shard", "ctx", None),
        P("shard", "ctx", None),
        P(),
        P(None, ("shard", "ctx")),
        P(None, ("shard", "ctx")),
        P(None, ("shard", "ctx")),
        P(("shard", "ctx"), None, "tp"),
        P(("shard", "ctx"), None, "tp"),
        P(("shard", "ctx"), None, "tp"),
        P(("shard", "ctx"), "tp"),
        P(("shard", "ctx"), "tp"),
        P(("shard", "ctx"), "tp"),
        P(("shard", "ctx"), "tp"),
        P(("shard", "ctx"), "tp"),
        P(("shard", "ctx"), "tp"),
        P(("shard", "ctx"), None, "tp"),
        P(("shard", "ctx"), None, "tp"),
        P(("shard", "ctx"), None, "tp"),
        P(("shard", "ctx"), "tp"),
        P(("shard", "ctx"), "tp"),
        P(("shard", "ctx"), "tp"),
        P(("shard", "ctx"), None, "tp"),
        P(("shard", "ctx"), None, "tp"),
        P(("shard", "ctx"), None, "tp"),
        P(("shard", "ctx"), "tp"),
        P(("shard", "ctx"), "tp"),
        P(("shard", "ctx"), "tp"),
    )
    return jax.shard_map(local, mesh=mesh, in_specs=in_specs, out_specs=out_specs, check_vma=False)
```

```python
import functools

import jax
import jax.numpy as jnp
from jax import lax
from jax.experimental import pallas as pl
from jax.experimental.layout import Layout, with_layout_constraint
from jax.experimental.pallas import tpu as pltpu
from jax.sharding import PartitionSpec as P

HD = 64
ROT = 32
STEP = 7
LANES = 128
MOST_BLOCKS = 8


norm_eps = 1e-05
clip_norm = 1.0
beta_first = 0.9
beta_second = 0.999
learn_rate = 0.03
gain_rate = 0.75
weight_decay = 0.01
adam_eps = 1e-08
masked_score = -1e30
bf = jnp.bfloat16
fl = jnp.float32
MIB = 1024 * 1024
SHORT = pl.CostEstimate(flops=1000, bytes_accessed=1000, transcendentals=0)


def params(mib):
    return pltpu.CompilerParams(vmem_limit_bytes=mib * MIB)


def whole(shape):
    return pl.BlockSpec(shape, lambda *index: (0,) * len(shape))


def matmul_t(left, right):
    return lax.dot_general(
        left, right, (((1,), (1,)), ((), ())), preferred_element_type=jnp.float32
    )


def matmul(left, right):
    return jnp.dot(left, right, preferred_element_type=jnp.float32)


def contract_rows(left, right):
    return lax.dot_general(
        left, right, (((0,), (0,)), ((), ())), preferred_element_type=jnp.float32
    )


def flip(block):
    return block.astype(fl).T


def norm_parts(rows):
    middle = jnp.mean(rows, axis=-1, keepdims=True)
    centred = rows - middle
    variance = jnp.mean(centred * centred, axis=-1, keepdims=True)
    inverse = lax.rsqrt(variance + norm_eps)
    return (centred * inverse, inverse)


def norm_back(grad_out, plain, inverse, gain):
    scaled = grad_out * gain
    term_mean = jnp.mean(scaled, axis=-1, keepdims=True)
    term_along = jnp.mean(scaled * plain, axis=-1, keepdims=True)
    return (inverse * (scaled - term_mean - plain * term_along), jnp.sum(grad_out * plain, axis=0))


def turn(lanes, cosine, sine_up, sine_down):
    return (
        lanes * cosine
        + pltpu.roll(lanes, ROT // 2, 1) * sine_up
        + pltpu.roll(lanes, LANES - ROT // 2, 1) * sine_down
    )


def pick(step, refs, held):
    for k, ref in enumerate(refs):

        @pl.when(step == k)
        def _(ref=ref):
            held[...] = ref[...]


def one_buffer(shape):
    return pl.BlockSpec(
        shape, lambda *index: (0,) * len(shape), pipeline_mode=pl.Buffered(buffer_count=1)
    )


def stacked(shape):
    return pl.BlockSpec((1,) + shape, lambda i: (i, 0, 0))


def project_kernel(count, few, scale, *refs):
    x_refs = refs[:count]
    gain_ref, w_ref, cos_ref, up_ref, down_ref, a_ref, qkv_ref, held = refs[count:]
    pick(pl.program_id(0), x_refs, held)
    plain, _ = norm_parts(held[...].astype(fl))
    rows = (plain * gain_ref[...]).astype(bf)
    a_ref[0] = rows
    projected = matmul(rows, w_ref[:, : 3 * few])
    cosine, up, down = cos_ref[0], up_ref[0], down_ref[0]
    lane = lax.broadcasted_iota(jnp.int32, cosine.shape, 1)
    for start in range(0, 2 * few, LANES):
        turned = turn(projected[:, start : start + LANES], cosine, up, down)
        if start < few:
            turned = jnp.where(lane < few - start, turned * scale, turned)
        qkv_ref[0, :, start : start + LANES] = turned.astype(bf)
    qkv_ref[0, :, 2 * few :] = projected[:, 2 * few :].astype(bf)


def project(blocks, gain, weight, tables, scale, few):
    count = len(blocks)
    rows, width = blocks[0].shape
    used = -(-3 * few // LANES) * LANES
    return pl.pallas_call(
        functools.partial(project_kernel, count, few, scale),
        grid=(count,),
        in_specs=[one_buffer((rows, width))] * count
        + [
            whole((1, width)),
            one_buffer((width, used)),
            stacked((rows, LANES)),
            stacked((rows, LANES)),
            stacked((rows, LANES)),
        ],
        out_specs=[stacked((rows, width)), stacked((rows, 3 * few))],
        out_shape=[
            jax.ShapeDtypeStruct((count, rows, width), bf),
            jax.ShapeDtypeStruct((count, rows, 3 * few), bf),
        ],
        scratch_shapes=[pltpu.VMEM((rows, width), bf)],
        compiler_params=params(48),
        cost_estimate=SHORT,
        name="project",
    )(*blocks, gain, weight, *(table.reshape(count, rows, LANES) for table in tables))


def attend_kernel(heads, wide, block, qkv_ref, mask_ref, o_ref, lse_ref):
    mask = mask_ref[:, 0:1] > 0.5
    total = qkv_ref.shape[0]
    for h in range(heads):
        low, high = h * HD, (h + 1) * HD
        keys = qkv_ref[:, wide + low : wide + high]
        values_t = flip(qkv_ref[:, 2 * wide + low : 2 * wide + high]).astype(bf)
        for b in range(total // block):
            queries = qkv_ref[b * block : (b + 1) * block, low:high]
            scores = jnp.where(mask, matmul_t(keys, queries), masked_score)
            peak = jnp.max(scores, axis=0, keepdims=True)
            weights = jnp.exp(scores - peak)
            sums = jnp.sum(weights, axis=0, keepdims=True)
            mixed = matmul(values_t, weights.astype(bf)) / sums
            o_ref[b * block : (b + 1) * block, low:high] = mixed.T.astype(bf)
            spot = h * (total // block) + b
            lse_ref[0, spot : spot + 1, :] = peak + jnp.log(sums)


def attend(qkv, mask, latents, heads, block):
    rows, lanes = qkv.shape
    wide = lanes // 3
    total = rows // latents
    spots = heads * (total // block)
    spots_up = -(-spots // 8) * 8
    return pl.pallas_call(
        functools.partial(attend_kernel, heads, wide, block),
        grid=(latents,),
        in_specs=[
            pl.BlockSpec((total, lanes), lambda i: (i, 0)),
            pl.BlockSpec((total, LANES), lambda i: (i, 0)),
        ],
        out_specs=[
            pl.BlockSpec((total, wide), lambda i: (i, 0)),
            pl.BlockSpec((1, spots_up, block), lambda i: (i, 0, 0)),
        ],
        out_shape=[
            jax.ShapeDtypeStruct((rows, wide), bf),
            jax.ShapeDtypeStruct((latents, spots_up, block), fl),
        ],
        compiler_params=params(48),
        cost_estimate=SHORT,
        name="attend",
    )(qkv, mask)


def attend_back_kernel(
    heads, wide, block, scale, qkv_ref, do_ref, o_ref, lse_ref, mask_ref, cos_ref, up_ref, down_ref,
    out_ref, work_ref,
):
    mask = mask_ref[:, 0:1] > 0.5
    total = qkv_ref.shape[0]
    ones = jnp.ones((8, HD), fl)
    for h in range(heads):
        low, high = h * HD, (h + 1) * HD
        keys = qkv_ref[:, wide + low : wide + high]
        keys_t = flip(keys).astype(bf)
        values = qkv_ref[:, 2 * wide + low : 2 * wide + high]
        grad_keys = jnp.zeros((total, HD), fl)
        grad_values = jnp.zeros((total, HD), fl)
        for b in range(total // block):
            queries = qkv_ref[b * block : (b + 1) * block, low:high]
            grads = do_ref[b * block : (b + 1) * block, low:high]
            mixed = o_ref[b * block : (b + 1) * block, low:high]
            spot = h * (total // block) + b
            scores = jnp.where(mask, matmul_t(keys, queries), masked_score)
            probs = jnp.exp(scores - lse_ref[0, spot : spot + 1, :])
            delta = lax.dot_general(
                ones,
                grads.astype(fl) * mixed.astype(fl),
                (((1,), (1,)), ((), ())),
                precision=lax.Precision.HIGHEST,
                preferred_element_type=fl,
            )[0:1]
            grad_scores = (probs * (matmul_t(values, grads) - delta)).astype(bf)
            grad_values += matmul(probs.astype(bf), grads)
            grad_keys += matmul(grad_scores, queries)
            grad_queries = matmul(keys_t, grad_scores) * scale
            work_ref[b * block : (b + 1) * block, low:high] = grad_queries.T
        work_ref[:, wide + low : wide + high] = grad_keys
        work_ref[:, 2 * wide + low : 2 * wide + high] = grad_values
    cosine, up, down = cos_ref[...], -up_ref[...], -down_ref[...]
    for start in range(0, 2 * wide, LANES):
        out_ref[:, start : start + LANES] = turn(
            work_ref[:, start : start + LANES], cosine, up, down
        ).astype(bf)
    out_ref[:, 2 * wide :] = work_ref[:, 2 * wide :].astype(bf)


def attend_back(qkv, grads, mixed, lse, mask, tables, latents, heads, block, scale):
    rows, lanes = qkv.shape
    wide = lanes // 3
    total = rows // latents
    by_latent = lambda n: pl.BlockSpec((total, n), lambda i: (i, 0))
    return pl.pallas_call(
        functools.partial(attend_back_kernel, heads, wide, block, scale),
        grid=(latents,),
        in_specs=[
            by_latent(lanes),
            by_latent(wide),
            by_latent(wide),
            pl.BlockSpec((1,) + lse.shape[1:], lambda i: (i, 0, 0)),
            by_latent(LANES),
            by_latent(LANES),
            by_latent(LANES),
            by_latent(LANES),
        ],
        out_specs=by_latent(lanes),
        out_shape=jax.ShapeDtypeStruct((rows, lanes), bf),
        scratch_shapes=[pltpu.VMEM((total, lanes), fl)],
        compiler_params=params(56),
        cost_estimate=SHORT,
        name="attend_back",
    )(qkv, grads, mixed, lse, mask, *tables)


def cross_kernel(heads, scale, q_ref, kv_ref, mask_ref, o_ref, lse_ref):
    mask = mask_ref[0, :, 0:1] > 0.5
    wide = heads * HD
    for first in range(0, heads, 2):
        pair = []
        for h in (first, first + 1):
            low, high = h * HD, (h + 1) * HD
            keys = kv_ref[0, :, low:high]
            values_t = flip(kv_ref[0, :, wide + low : wide + high]).astype(bf)
            scores = jnp.where(mask, matmul_t(keys, q_ref[0, :, low:high]) * scale, masked_score)
            peak = jnp.max(scores, axis=0, keepdims=True)
            weights = jnp.exp(scores - peak)
            sums = jnp.sum(weights, axis=0, keepdims=True)
            pair.append(matmul(values_t, weights.astype(bf)) / sums)
            lse_ref[0, h : h + 1, :] = peak + jnp.log(sums)
        o_ref[0, :, first * HD : (first + 2) * HD] = (
            jnp.concatenate(pair, axis=0).T.astype(bf)
        )


def cross(queries, pairs, mask, scale):
    latents, rows, wide = queries.shape
    heads = wide // HD
    heads_up = -(-heads // 8) * 8
    one = lambda shape: pl.BlockSpec((1,) + shape, lambda i: (i, 0, 0))
    return pl.pallas_call(
        functools.partial(cross_kernel, heads, scale),
        grid=(latents,),
        in_specs=[one((rows, wide)), one(pairs.shape[1:]), one(mask.shape[1:])],
        out_specs=[one((rows, wide)), one((heads_up, rows))],
        out_shape=[
            jax.ShapeDtypeStruct((latents, rows, wide), bf),
            jax.ShapeDtypeStruct((latents, heads_up, rows), fl),
        ],
        compiler_params=params(32),
        cost_estimate=SHORT,
        name="cross",
    )(queries, pairs, mask)


def cross_back_kernel(
    heads, scale, q_ref, kv_ref, do_ref, o_ref, lse_ref, mask_ref, dq_ref, dkv_ref
):
    mask = mask_ref[0, :, 0:1] > 0.5
    wide = heads * HD
    ones = jnp.ones((8, HD), fl)
    for first in range(0, heads, 2):
        pair = []
        grad_keys = []
        grad_values = []
        for h in (first, first + 1):
            low, high = h * HD, (h + 1) * HD
            keys = kv_ref[0, :, low:high]
            keys_t = flip(keys).astype(bf)
            values = kv_ref[0, :, wide + low : wide + high]
            queries = q_ref[0, :, low:high]
            grads = do_ref[0, :, low:high]
            scores = jnp.where(mask, matmul_t(keys, queries) * scale, masked_score)
            probs = jnp.exp(scores - lse_ref[0, h : h + 1, :])
            delta = lax.dot_general(
                ones,
                grads.astype(fl) * o_ref[0, :, low:high].astype(fl),
                (((1,), (1,)), ((), ())),
                precision=lax.Precision.HIGHEST,
                preferred_element_type=fl,
            )[0:1]
            grad_scores = (probs * (matmul_t(values, grads) - delta)).astype(bf)
            grad_values.append(matmul(probs.astype(bf), grads))
            grad_keys.append(matmul(grad_scores, queries) * scale)
            pair.append(matmul(keys_t, grad_scores) * scale)
        low, high = first * HD, (first + 2) * HD
        dq_ref[0, :, low:high] = jnp.concatenate(pair, axis=0).T.astype(bf)
        dkv_ref[0, :, low:high] = jnp.concatenate(grad_keys, axis=1).astype(bf)
        dkv_ref[0, :, wide + low : wide + high] = jnp.concatenate(grad_values, axis=1).astype(bf)


def cross_back(queries, pairs, grads, mixed, lse, mask, scale):
    latents, rows, wide = queries.shape
    heads = wide // HD
    one = lambda shape: pl.BlockSpec((1,) + shape, lambda i: (i, 0, 0))
    return pl.pallas_call(
        functools.partial(cross_back_kernel, heads, scale),
        grid=(latents,),
        in_specs=[
            one((rows, wide)),
            one(pairs.shape[1:]),
            one((rows, wide)),
            one((rows, wide)),
            one(lse.shape[1:]),
            one(mask.shape[1:]),
        ],
        out_specs=[one((rows, wide)), one(pairs.shape[1:])],
        out_shape=[
            jax.ShapeDtypeStruct(queries.shape, bf),
            jax.ShapeDtypeStruct(pairs.shape, bf),
        ],
        compiler_params=params(32),
        cost_estimate=SHORT,
        name="cross_back",
    )(queries, pairs, grads, mixed, lse, mask)


def mix_back_kernel(count, *refs):
    g_refs = refs[:count]
    w_ref, o_ref, do_ref, grad_ref, held, total = refs[count:]
    step = pl.program_id(0)
    few = o_ref.shape[2]

    @pl.when(step == 0)
    def _():
        total[...] = jnp.zeros_like(total)

    pick(step, g_refs, held)
    rows = held[...]
    do_ref[0] = matmul(rows, w_ref[:, :few]).astype(bf)
    total[...] += matmul(flip(o_ref[0]).astype(bf), rows)

    @pl.when(step == count - 1)
    def _():
        grad_ref[...] = total[...].T.astype(bf)


def mix_back(blocks, weight, mixed):
    count = len(blocks)
    rows, width = blocks[0].shape
    few = mixed.shape[2]
    return pl.pallas_call(
        functools.partial(mix_back_kernel, count),
        grid=(count,),
        in_specs=[one_buffer((rows, width))] * count
        + [one_buffer(weight.shape), stacked((rows, few))],
        out_specs=[stacked((rows, few)), whole((width, few))],
        out_shape=[
            jax.ShapeDtypeStruct((count, rows, few), bf),
            jax.ShapeDtypeStruct((width, few), bf),
        ],
        scratch_shapes=[pltpu.VMEM((rows, width), bf), pltpu.VMEM((few, width), fl)],
        compiler_params=params(48),
        cost_estimate=SHORT,
        name="mix_back",
    )(*blocks, weight, mixed)


def mlp_kernel(count, given, *refs):
    a_refs, dy_refs = refs[:given], refs[given : 2 * given]
    (
        gate_ref,
        up_ref,
        down_ref,
        a_ref,
        dy_ref,
        h_ref,
        dgu_ref,
        out_other,
        out_own,
        da_other,
        da_own,
        weight,
        a_held,
        dy_held,
    ) = refs[2 * given :]
    step = pl.program_id(0)
    ctxs, shards, owned, units = gate_ref.shape

    @pl.when(step == 0)
    def _():
        for s in range(shards):
            for c in range(ctxs):
                row = (s * ctxs + c) * owned
                for k, kind in enumerate((gate_ref, up_ref, down_ref)):
                    weight[row : row + owned, k * units : (k + 1) * units] = kind[c, s]

    if given == count:
        pick(step, a_refs, a_held)
        pick(step, dy_refs, dy_held)
    else:
        a_held[...] = a_refs[0][0]
        dy_held[...] = dy_refs[0][0]
    rows = a_held[...]
    grads = dy_held[...]
    a_ref[0] = rows
    dy_ref[0] = grads
    gate = matmul(rows, weight[:, :units])
    upward = matmul(rows, weight[:, units : 2 * units])
    sigmoid = jax.nn.sigmoid(gate)
    activated = gate * sigmoid
    hidden = (activated * upward).astype(bf)
    h_ref[0] = hidden
    grad_hidden = matmul(grads, weight[:, 2 * units :])
    grad_gate = (grad_hidden * upward * sigmoid * (1.0 + gate * (1.0 - sigmoid))).astype(bf)
    grad_up = (grad_hidden * activated).astype(bf)
    dgu_ref[0, :, :units] = grad_gate
    dgu_ref[0, :, units:] = grad_up
    da = (
        matmul_t(grad_gate, weight[:, :units]) + matmul_t(grad_up, weight[:, units : 2 * units])
    ).astype(bf)
    out = matmul_t(hidden, weight[:, 2 * units :]).astype(bf)

    @pl.when(step < count // 2)
    def _():
        da_other[0] = da
        out_other[0] = out

    @pl.when(step >= count // 2)
    def _():
        da_own[0] = da
        out_own[0] = out


def mlp(blocks, grads, weights):
    count = len(blocks)
    half = count // 2
    rows, width = blocks[0].shape
    units = weights[0].shape[3]
    if count <= MOST_BLOCKS:
        feeds = one_buffer((rows, width))
    else:
        feeds = stacked((rows, width))
        blocks, grads = [jnp.stack(blocks)], [jnp.stack(grads)]
    given = len(blocks)
    first = pl.BlockSpec((1, rows, width), lambda i: (jnp.minimum(i, half - 1), 0, 0))
    second = pl.BlockSpec((1, rows, width), lambda i: (jnp.maximum(i - half, 0), 0, 0))
    return pl.pallas_call(
        functools.partial(mlp_kernel, count, given),
        grid=(count,),
        in_specs=[feeds] * (2 * given) + [one_buffer(weights[0].shape)] * 3,
        out_specs=[
            stacked((rows, width)),
            stacked((rows, width)),
            stacked((rows, units)),
            stacked((rows, 2 * units)),
            first,
            second,
            first,
            second,
        ],
        out_shape=[
            jax.ShapeDtypeStruct((count, rows, width), bf),
            jax.ShapeDtypeStruct((count, rows, width), bf),
            jax.ShapeDtypeStruct((count, rows, units), bf),
            jax.ShapeDtypeStruct((count, rows, 2 * units), bf),
        ]
        + [jax.ShapeDtypeStruct((half, rows, width), bf)] * 4,
        scratch_shapes=[
            pltpu.VMEM((width, 3 * units), bf),
            pltpu.VMEM((rows, width), bf),
            pltpu.VMEM((rows, width), bf),
        ],
        compiler_params=params(60),
        cost_estimate=SHORT,
        name="mlp",
    )(*blocks, *grads, *weights)


def after(value, *others):
    return lax.optimization_barrier((value,) + others)[0] if others else value


def swap(value):
    return lax.ppermute(value, "tp", [(0, 1), (1, 0)])


def ring_shift(value, by):
    size = lax.axis_size("ctx")
    return lax.ppermute(value, "ctx", [(i, (i - by) % size) for i in range(size)])


def cross_over(value, bits):
    size = lax.axis_size("shard")
    return lax.ppermute(value, "shard", [(i, i ^ bits) for i in range(size)])


def together(values, *others):
    return lax.optimization_barrier((tuple(values),) + others)[0]


def nothing(token):
    return ()


def ring_gather(own, first=(), second=()):
    size = lax.axis_size("ctx")
    if size != 4:
        return [own] + [after(ring_shift(own, r), *second) for r in range(1, size)]
    half = own.shape[-1] // 2
    following, before = together((ring_shift(own, 1), ring_shift(own, -1)), *first)
    far = together(
        (ring_shift(following[:, :half], 1), ring_shift(before[:, half:], -1)), *second
    )
    return [own, following, jnp.concatenate(far, axis=-1), before]


def ring_scatter(parts, first=(), between=nothing):
    if lax.axis_size("ctx") != 4:
        total = parts[0].astype(fl)
        for r in range(1, len(parts)):
            total = total + after(ring_shift(parts[r], -r), *between(parts[0])).astype(fl)
        return total
    half = parts[0].shape[-1] // 2
    by_after, by_before = together(
        (ring_shift(parts[2][:, :half], -1), ring_shift(parts[2][:, half:], 1)), *first
    )
    to_after = jnp.concatenate([parts[1][:, :half] + by_after, parts[1][:, half:]], axis=-1)
    to_before = jnp.concatenate([parts[3][:, :half], parts[3][:, half:] + by_before], axis=-1)
    from_before, from_after = together(
        (ring_shift(to_after, -1), ring_shift(to_before, 1)), *between(by_after)
    )
    return parts[0].astype(fl) + from_before.astype(fl) + from_after.astype(fl)


def ring_exchange(parts, before=()):
    return [parts[0]] + [after(ring_shift(part, -r), *before) for r, part in enumerate(parts[1:], 1)]


def square_exchange(parts, before=()):
    return [parts[0]] + [after(cross_over(part, r), *before) for r, part in enumerate(parts[1:], 1)]


def summed(parts):
    total = parts[0].astype(fl)
    for part in parts[1:]:
        total = total + part.astype(fl)
    return total


def at(array, index):
    return lax.dynamic_index_in_dim(array, index, 0, keepdims=False)


def rows_at(array, index, count):
    return lax.dynamic_slice_in_dim(array, index * count, count, 0)


def place(blocks, indices):
    out = jnp.zeros((len(blocks),) + blocks[0].shape, blocks[0].dtype)
    for block, index in zip(blocks, indices):
        out = lax.dynamic_update_index_in_dim(out, block, index, 0)
    return out


def square_gather(own, first=(), second=()):
    size = lax.axis_size("shard")
    if size != 4:
        return [own] + [after(cross_over(own, r), *second) for r in range(1, size)]
    half = own.shape[-1] // 2
    one, two = together((cross_over(own, 1), cross_over(own, 2)), *first)
    three = together((cross_over(two[:, :half], 1), cross_over(one[:, half:], 2)), *second)
    return [own, one, two, jnp.concatenate(three, axis=-1)]


def square_scatter(parts, first=(), between=nothing):
    size = lax.axis_size("shard")
    if size != 4:
        total = parts[0].astype(fl)
        for r in range(1, size):
            total = total + after(cross_over(parts[r], r), *between(parts[0])).astype(fl)
        return total
    half = parts[0].shape[-1] // 2
    by_one, by_two = together(
        (cross_over(parts[3][:, :half], 1), cross_over(parts[3][:, half:], 2)), *first
    )
    to_two = jnp.concatenate([parts[2][:, :half] + by_one, parts[2][:, half:]], axis=-1)
    to_one = jnp.concatenate([parts[1][:, :half], parts[1][:, half:] + by_two], axis=-1)
    from_one, from_two = together(
        (cross_over(to_one, 1), cross_over(to_two, 2)), *between(by_one)
    )
    return parts[0].astype(fl) + from_one.astype(fl) + from_two.astype(fl)


def total_over_all(value):
    for axis in ("tp", "shard", "ctx"):
        size = lax.axis_size(axis)
        bit = 1
        while bit < size:
            value = value + lax.ppermute(value, axis, [(i, i ^ bit) for i in range(size)])
            bit *= 2
    return value


def adam_step(weight, moment, square, grad, scale, decay, rate):
    grad = grad * scale
    moment_new = beta_first * moment + (1.0 - beta_first) * grad
    square_new = beta_second * square + (1.0 - beta_second) * grad * grad
    moment_hat = moment_new / (1.0 - beta_first**STEP)
    square_hat = square_new / (1.0 - beta_second**STEP)
    weight_new = weight - rate * (moment_hat / (jnp.sqrt(square_hat) + adam_eps) + decay * weight)
    return (moment_new, square_new, weight_new)


def rotary_tables(positions):
    lane = jnp.arange(LANES, dtype=jnp.int32) % HD
    step = (lane % (ROT // 2)).astype(fl) * 2.0 / ROT
    frequency = jnp.where(lane < ROT, 10000.0 ** (-step), 0.0)
    angles = positions.astype(fl)[:, None] * frequency[None, :]
    sine = jnp.sin(angles)
    up = jnp.where((lane >= ROT // 2) & (lane < ROT), sine, 0.0)
    down = jnp.where(lane < ROT // 2, -sine, 0.0)
    return (jnp.cos(angles), up, down)


def local(
    tokens,
    conditioning,
    cotangent,
    piece_lengths,
    start_positions,
    cond_counts,
    norm_gains,
    gains_moment,
    gains_square,
    qkv_weight,
    qkv_moment,
    qkv_square,
    output_weight,
    output_moment,
    output_square,
    cross_query_weight,
    cross_query_moment,
    cross_query_square,
    cross_pair_weight,
    cross_pair_moment,
    cross_pair_square,
    cross_out_weight,
    cross_out_moment,
    cross_out_square,
    gate_up_weight,
    gate_up_moment,
    gate_up_square,
    down_weight,
    down_moment,
    down_square,
):
    seqs, cap, width = tokens.shape
    cond_len = conditioning.shape[1]
    pieces = piece_lengths.shape[1]
    scale = HD ** (-0.5)
    shards = lax.axis_size("shard")
    ctxs = lax.axis_size("ctx")
    shard_index = lax.axis_index("shard")
    ctx_index = lax.axis_index("ctx")
    tp_index = lax.axis_index("tp")
    owned = qkv_weight.shape[0]
    local_width = qkv_weight.shape[2]
    units_half = down_weight.shape[1]
    few = local_width // ctxs
    heads_few = few // HD
    units = units_half // shards

    latent_order = (tp_index + jnp.arange(seqs, dtype=jnp.int32)) % seqs
    piece_order = (ctx_index + jnp.arange(pieces, dtype=jnp.int32)) % pieces
    mine = lambda array: lax.dynamic_index_in_dim(array, latent_order[0], 0, keepdims=False)
    others = lambda array: lax.dynamic_index_in_dim(array, latent_order[1], 0, keepdims=False)

    def both(array):
        return jnp.stack([mine(array), others(array)])

    offsets = jnp.cumsum(piece_lengths, axis=1) - piece_lengths
    slot = jnp.arange(cap, dtype=jnp.int32)
    lengths_here = both(piece_lengths)[:, piece_order]
    offsets_here = both(offsets)[:, piece_order]
    starts_here = both(start_positions)
    positions = (starts_here[:, None, None] + offsets_here[:, :, None] + slot).reshape(-1)
    key_valid = (slot < lengths_here[:, :, None]).reshape(-1)
    key_mask = jnp.broadcast_to(key_valid.astype(fl)[:, None], (key_valid.shape[0], LANES))
    tables = lax.optimization_barrier(rotary_tables(positions))
    other_valid = (slot < lengths_here[1, 0]).astype(fl)[:, None]
    own_valid = (slot < lengths_here[0, 0]).astype(fl)[:, None]

    tokens_mine = mine(tokens)
    tokens_other = others(tokens)
    dy_mine = mine(cotangent).astype(fl) * own_valid
    dy_low = dy_mine.astype(bf)

    kinds = jnp.concatenate(
        [
            qkv_weight.astype(bf),
            output_weight.astype(bf)[:, None],
            cross_pair_weight.astype(bf),
        ],
        axis=1,
    )
    n_kinds = kinds.shape[1]
    kinds = jnp.transpose(kinds.reshape(owned, n_kinds, ctxs, few), (2, 0, 1, 3)).reshape(
        ctxs, owned, n_kinds * few
    )
    gain_lanes = jnp.pad(jnp.transpose(norm_gains).astype(bf), ((0, 0), (0, LANES - 3)))
    sent_attn = jnp.concatenate(
        [kinds, jnp.broadcast_to(gain_lanes[None], (ctxs, owned, LANES))], axis=2
    )
    sent_attn = after(sent_attn, tokens_mine)
    ctx_after = [(ctx_index + r) % ctxs for r in range(ctxs)]
    ctx_before = [(ctx_index - r) % ctxs for r in range(ctxs)]
    shard_near = [shard_index ^ r for r in range(shards)]
    sent_mlp = jnp.concatenate(
        [
            gate_up_weight.astype(bf),
            down_weight.astype(bf)[:, None],
        ],
        axis=1,
    )
    sent_mlp = jnp.transpose(sent_mlp.reshape(owned, 3, shards, units), (2, 0, 1, 3)).reshape(
        shards, owned, 3 * units
    )
    attn_rows = after(
        lax.all_to_all(sent_attn, "ctx", 0, 0, tiled=True), sent_mlp, *tables
    ).reshape(ctxs * owned, -1)
    attn_full = lax.all_gather(attn_rows, "shard", axis=0, tiled=True)
    pair_full = attn_full[:, 4 * few : 6 * few]
    output_full = attn_full[:, 3 * few : 4 * few]
    gains = jnp.transpose(attn_full[:, n_kinds * few : n_kinds * few + 3].astype(fl))

    token_blocks = ring_gather(tokens_mine, (attn_rows,))
    sent_mlp = lax.all_to_all(sent_mlp, "shard", 0, 0, tiled=True)
    sent_gate, sent_up, sent_down = (
        sent_mlp[:, :, k * units : (k + 1) * units] for k in range(3)
    )
    over_ctx = lambda array: lax.all_gather(array, "ctx", axis=0, tiled=False)
    token_swapped = [tokens_other] + [swap(block) for block in token_blocks[1:]]
    token_last = after(token_swapped[-1], sent_gate, sent_up, sent_down)

    total = pieces * cap
    block = total // 3
    input1, qkv = project(
        token_blocks + token_swapped[:-1] + [token_last], gains[0:1], attn_full, tables, scale, few
    )
    qkv = qkv.reshape(seqs * total, 3 * few)
    cond_up = -(-cond_len // 16) * 16
    cond_rows = jnp.pad(both(conditioning), ((0, 0), (0, cond_up - cond_len), (0, 0))).reshape(
        seqs * cond_up, width
    )
    own_pairs = matmul(cond_rows, pair_full).astype(bf)
    gate_full = over_ctx(after(sent_gate, token_last, attn_full))
    sent_cross = jnp.concatenate(
        [cross_query_weight.astype(bf), cross_out_weight.astype(bf)], axis=1
    )
    sent_cross = after(sent_cross, qkv)
    cross_rows = [sent_cross] + [ring_shift(sent_cross, r) for r in range(1, ctxs)]
    mixed_low, lse = attend(qkv, key_mask, seqs, heads_few, block)
    cross_rows = place(cross_rows, ctx_after).reshape(ctxs * owned, -1)
    cross_full = lax.all_gather(after(cross_rows, gate_full), "shard", axis=0, tiled=True)
    partial = matmul_t(mixed_low, output_full).astype(bf).reshape(seqs, pieces, cap, width)
    from_other = swap(partial[1])
    mine_parts = [partial[0, r] + from_other[r] for r in range(pieces)]
    own_pairs = after(own_pairs, mixed_low)
    pairs = [own_pairs] + [ring_shift(own_pairs, r) for r in range(1, ctxs)]
    pairs = place(pairs, ctx_after)
    pairs = jnp.transpose(
        pairs.reshape(ctxs, seqs, cond_up, 2, few), (1, 2, 3, 0, 4)
    ).reshape(seqs, cond_up, 2 * local_width)
    query_full = cross_full[:, :local_width]
    cross_out_full = cross_full[:, local_width:]
    x_rows = tokens_mine.astype(fl)
    x_first = x_rows + ring_scatter(mine_parts, (cross_rows,), lambda token: (pairs,))
    up_full = over_ctx(after(sent_up, x_first))
    down_full = over_ctx(after(sent_down, x_first))
    dy_low = after(dy_low, x_first)
    dy_blocks = [dy_low] + [cross_over(dy_low, r) for r in range(1, shards)]
    dy_other = (others(cotangent).astype(fl) * other_valid).astype(bf)
    dy_swapped = [dy_other] + [swap(block_of) for block_of in dy_blocks[1:]]

    plain2, inverse2 = norm_parts(x_first)
    input2_mine = (plain2 * gains[1]).astype(bf)
    input2 = jnp.concatenate([input2_mine, swap(input2_mine)], axis=0)
    cross_queries = matmul(input2, query_full).astype(bf).reshape(seqs, cap, local_width)
    cond_valid = jnp.arange(cond_up, dtype=jnp.int32)[None, :] < both(cond_counts)[:, None]
    cond_mask = jnp.broadcast_to(cond_valid.astype(fl)[:, :, None], (seqs, cond_up, LANES))
    cross_low, cross_lse = cross(cross_queries, pairs, cond_mask, scale)
    cross_low_rows = cross_low.reshape(seqs * cap, local_width)
    cross_partial = matmul_t(cross_low_rows, cross_out_full).astype(bf)
    x_second = x_first + (
        cross_partial[:cap].astype(fl) + swap(cross_partial[cap:]).astype(fl)
    )

    plain3, inverse3 = norm_parts(x_second)
    input3 = (plain3 * gains[2]).astype(bf)
    input3_blocks = square_gather(input3, (), dy_swapped)
    (
        input3_all,
        dy_all,
        hidden,
        grad_gated,
        down_other,
        down_own,
        back_other,
        back_own,
    ) = mlp(
        [swap(block_of) for block_of in input3_blocks] + input3_blocks,
        dy_swapped + dy_blocks,
        (gate_full, up_full, down_full),
    )
    merged = lambda array: array.reshape(-1, array.shape[-1])
    grad_down = contract_rows(merged(dy_all), merged(hidden)).astype(bf)
    grad_gate = contract_rows(merged(input3_all), merged(grad_gated)[:, :units]).astype(bf)
    grad_up = contract_rows(merged(input3_all), merged(grad_gated)[:, units:]).astype(bf)

    def add_cores(own, other):
        from_other = swap(other)
        return [own[r] + from_other[r] for r in range(own.shape[0])]

    def by_owner(array):
        return jnp.transpose(
            array.reshape(shards, ctxs, owned, array.shape[1]), (1, 0, 2, 3)
        ).reshape(ctxs * shards * owned, -1)

    def sum_over_ctx(array):
        return lax.psum_scatter(array, "ctx", scatter_dimension=0, tiled=True)

    grad_down, grad_gate, grad_up = by_owner(grad_down), by_owner(grad_gate), by_owner(grad_up)
    back_sum = square_scatter(
        add_cores(back_own, back_other), (grad_down,), lambda token: (grad_gate, grad_up)
    )
    back3, grad_gain3 = norm_back(back_sum, plain3, inverse3, gains[2])

    def natural(first, second):
        straight = tp_index == 0
        return jnp.stack(
            [jnp.where(straight, first, second), jnp.where(straight, second, first)]
        )

    sum_down = sum_over_ctx(grad_down)
    sum_gate = sum_over_ctx(grad_gate)

    grad_second = dy_mine + back3
    grad2_mine = grad_second.astype(bf)
    grad2_low = jnp.concatenate([grad2_mine, swap(grad2_mine)], axis=0)
    grad_cross_out = contract_rows(grad2_low, cross_low_rows)
    grad_cmixed = matmul(grad2_low, cross_out_full).astype(bf).reshape(seqs, cap, local_width)
    grad_cq, grad_pairs = cross_back(
        cross_queries, pairs, grad_cmixed, cross_low, cross_lse, cond_mask, scale
    )
    grad_cq = grad_cq.reshape(seqs * cap, local_width)
    grad_query = contract_rows(input2, grad_cq)
    query_partial = matmul_t(grad_cq, query_full).astype(bf)
    back2, grad_gain2 = norm_back(
        query_partial[:cap].astype(fl) + swap(query_partial[cap:]).astype(fl),
        plain2,
        inverse2,
        gains[1],
    )
    grad_cross = jnp.concatenate([grad_query.astype(bf), grad_cross_out.astype(bf)], axis=1)
    grad_pairs = jnp.transpose(
        grad_pairs.reshape(seqs, cond_up, 2, ctxs, few), (3, 0, 1, 2, 4)
    ).reshape(ctxs, seqs * cond_up, 2 * few)

    grad_first = grad_second + back2
    grad1_mine = grad_first.astype(bf)
    down_parts = add_cores(after(down_own, back_sum), after(down_other, back_sum))
    down_sum = summed(square_exchange(down_parts, (grad1_mine,)))
    block_mine = (x_second + down_sum).astype(bf)
    block_out = natural(block_mine, swap(block_mine))
    grad1_blocks = ring_gather(
        grad1_mine, (grad_cross, grad_pairs, sum_down), (block_mine, sum_gate)
    )
    cross_sum = lax.psum_scatter(
        after(grad_cross, grad1_mine), "shard", scatter_dimension=0, tiled=True
    )
    grad_mixed, grad_output = mix_back(
        grad1_blocks + [swap(block_of) for block_of in grad1_blocks],
        output_full,
        mixed_low.reshape(seqs * pieces, cap, few),
    )
    sum_up = sum_over_ctx(after(grad_up, grad1_blocks[2]))
    grad_pairs = after(grad_pairs, grad_mixed)
    own_pair_grads = summed(
        ring_exchange([at(grad_pairs, index) for index in ctx_after])
    ).astype(bf)
    grad_pair = contract_rows(cond_rows, own_pair_grads).astype(bf)
    to_owner = lambda array: jnp.transpose(
        lax.all_to_all(array.reshape(shards, owned, -1), "shard", 0, 0, tiled=True), (1, 0, 2)
    ).reshape(owned, units_half)
    own_gate = to_owner(after(sum_gate, grad_mixed))
    own_down = to_owner(after(sum_down, grad_mixed))
    grad_projected = attend_back(
        qkv,
        grad_mixed.reshape(seqs * total, few),
        mixed_low,
        lse,
        key_mask,
        tables,
        seqs,
        heads_few,
        block,
        scale,
    )
    grad_turned = after(grad_projected, own_gate, own_down, grad_pair, cross_sum)
    grad_qkv = contract_rows(merged(input1), grad_turned).astype(bf)
    grad_attn = jnp.concatenate([grad_qkv, grad_output, grad_pair], axis=1)
    attn_sum = lax.psum_scatter(grad_attn, "shard", scatter_dimension=0, tiled=True)
    first_partial = matmul_t(after(grad_turned, grad_attn, sum_up), attn_full[:, : 3 * few]).astype(
        bf
    ).reshape(seqs, pieces, cap, width)
    first_parts = add_cores(first_partial[0], first_partial[1])
    arrived = []

    def exchange(token):
        arrived.extend(
            [
                to_owner(after(sum_up, token)),
                summed(
                    ring_exchange(
                        [rows_at(after(cross_sum, token), index, owned) for index in ctx_after]
                    )
                ),
            ]
        )
        return arrived

    back1_sum = ring_scatter(first_parts, (), exchange)
    own_up = arrived[0]
    own_cross = arrived[1]
    plain1, inverse1 = norm_parts(x_rows)
    back1, grad_gain1 = norm_back(back1_sum, plain1, inverse1, gains[0])
    tokens_grad_mine = grad_first + back1
    tokens_grad = natural(tokens_grad_mine, swap(tokens_grad_mine))

    own_kinds = lax.all_to_all(attn_sum.reshape(ctxs, owned, -1), "ctx", 0, 0, tiled=True)
    own_kinds = jnp.transpose(
        own_kinds.reshape(ctxs, owned, n_kinds, few), (1, 2, 0, 3)
    ).reshape(owned, n_kinds, local_width).astype(fl)
    own_qkv = own_kinds[:, :3]
    own_output = own_kinds[:, 3]
    own_pair = own_kinds[:, 4:]
    own_query = own_cross[:, :local_width]
    own_cross_out = own_cross[:, local_width:]
    own_gate_up = with_layout_constraint(
        jnp.stack([own_gate, own_up], axis=1), Layout((0, 1, 2))
    ).astype(fl)
    own_down = own_down.astype(fl)

    squares = jnp.sum(own_kinds * own_kinds) + jnp.sum(own_cross * own_cross)
    squares = squares + jnp.sum(own_gate_up * own_gate_up) + jnp.sum(own_down * own_down)
    totals = total_over_all(
        jnp.concatenate(
            [
                jnp.stack([grad_gain1, grad_gain2, grad_gain3]),
                jnp.broadcast_to(squares, (5, width)),
            ]
        )
    )
    gain_grads = totals[:3]
    own_gains = lax.dynamic_slice_in_dim(
        gain_grads, (shard_index * ctxs + ctx_index) * owned, owned, 1
    )
    grad_norm = jnp.sqrt(totals[3, 0] + jnp.sum(gain_grads * gain_grads))
    clip_scale = clip_norm / jnp.maximum(grad_norm, clip_norm)

    def step(weight, moment, square, grad):
        return adam_step(weight, moment, square, grad, clip_scale, weight_decay, learn_rate)

    return (
        block_out,
        tokens_grad,
        grad_norm,
        *adam_step(
            norm_gains, gains_moment, gains_square, own_gains, clip_scale, 0.0, gain_rate
        ),
        *step(qkv_weight, qkv_moment, qkv_square, own_qkv),
        *step(output_weight, output_moment, output_square, own_output),
        *step(cross_query_weight, cross_query_moment, cross_query_square, own_query),
        *step(cross_pair_weight, cross_pair_moment, cross_pair_square, own_pair),
        *step(cross_out_weight, cross_out_moment, cross_out_square, own_cross_out),
        *step(gate_up_weight, gate_up_moment, gate_up_square, own_gate_up),
        *step(down_weight, down_moment, down_square, own_down),
    )


def solution(mesh):
    in_specs = (
        P("shard", "ctx", None),
        P("shard", None, None),
        P("shard", "ctx", None),
        P("shard", None),
        P("shard"),
        P("shard"),
        P(None, ("shard", "ctx")),
        P(None, ("shard", "ctx")),
        P(None, ("shard", "ctx")),
        P(("shard", "ctx"), None, "tp"),
        P(("shard", "ctx"), None, "tp"),
        P(("shard", "ctx"), None, "tp"),
        P(("shard", "ctx"), "tp"),
        P(("shard", "ctx"), "tp"),
        P(("shard", "ctx"), "tp"),
        P(("shard", "ctx"), "tp"),
        P(("shard", "ctx"), "tp"),
        P(("shard", "ctx"), "tp"),
        P(("shard", "ctx"), None, "tp"),
        P(("shard", "ctx"), None, "tp"),
        P(("shard", "ctx"), None, "tp"),
        P(("shard", "ctx"), "tp"),
        P(("shard", "ctx"), "tp"),
        P(("shard", "ctx"), "tp"),
        P(("shard", "ctx"), None, "tp"),
        P(("shard", "ctx"), None, "tp"),
        P(("shard", "ctx"), None, "tp"),
        P(("shard", "ctx"), "tp"),
        P(("shard", "ctx"), "tp"),
        P(("shard", "ctx"), "tp"),
    )
    out_specs = (
        P("shard", "ctx", None),
        P("shard", "ctx", None),
        P(),
        P(None, ("shard", "ctx")),
        P(None, ("shard", "ctx")),
        P(None, ("shard", "ctx")),
        P(("shard", "ctx"), None, "tp"),
        P(("shard", "ctx"), None, "tp"),
        P(("shard", "ctx"), None, "tp"),
        P(("shard", "ctx"), "tp"),
        P(("shard", "ctx"), "tp"),
        P(("shard", "ctx"), "tp"),
        P(("shard", "ctx"), "tp"),
        P(("shard", "ctx"), "tp"),
        P(("shard", "ctx"), "tp"),
        P(("shard", "ctx"), None, "tp"),
        P(("shard", "ctx"), None, "tp"),
        P(("shard", "ctx"), None, "tp"),
        P(("shard", "ctx"), "tp"),
        P(("shard", "ctx"), "tp"),
        P(("shard", "ctx"), "tp"),
        P(("shard", "ctx"), None, "tp"),
        P(("shard", "ctx"), None, "tp"),
        P(("shard", "ctx"), None, "tp"),
        P(("shard", "ctx"), "tp"),
        P(("shard", "ctx"), "tp"),
        P(("shard", "ctx"), "tp"),
    )
    return jax.shard_map(local, mesh=mesh, in_specs=in_specs, out_specs=out_specs, check_vma=False)
```

```python
import functools

import jax
import jax.numpy as jnp
from jax import lax
from jax.experimental import pallas as pl
from jax.experimental.layout import Layout, with_layout_constraint
from jax.experimental.pallas import tpu as pltpu
from jax.sharding import PartitionSpec as P

HD = 64
ROT = 32
STEP = 7
LANES = 128
MOST_BLOCKS = 8


norm_eps = 1e-05
clip_norm = 1.0
beta_first = 0.9
beta_second = 0.999
learn_rate = 0.03
gain_rate = 0.75
weight_decay = 0.01
adam_eps = 1e-08
masked_score = -1e30
bf = jnp.bfloat16
fl = jnp.float32
MIB = 1024 * 1024
SHORT = pl.CostEstimate(flops=1000, bytes_accessed=1000, transcendentals=0)


def params(mib):
    return pltpu.CompilerParams(vmem_limit_bytes=mib * MIB)


def whole(shape):
    return pl.BlockSpec(shape, lambda *index: (0,) * len(shape))


def matmul_t(left, right):
    return lax.dot_general(
        left, right, (((1,), (1,)), ((), ())), preferred_element_type=jnp.float32
    )


def matmul(left, right):
    return jnp.dot(left, right, preferred_element_type=jnp.float32)


def contract_rows(left, right):
    return lax.dot_general(
        left, right, (((0,), (0,)), ((), ())), preferred_element_type=jnp.float32
    )


def flip(block):
    return block.astype(fl).T


def norm_parts(rows):
    middle = jnp.mean(rows, axis=-1, keepdims=True)
    centred = rows - middle
    variance = jnp.mean(centred * centred, axis=-1, keepdims=True)
    inverse = lax.rsqrt(variance + norm_eps)
    return (centred * inverse, inverse)


def norm_back(grad_out, plain, inverse, gain):
    scaled = grad_out * gain
    term_mean = jnp.mean(scaled, axis=-1, keepdims=True)
    term_along = jnp.mean(scaled * plain, axis=-1, keepdims=True)
    return (inverse * (scaled - term_mean - plain * term_along), jnp.sum(grad_out * plain, axis=0))


def turn(lanes, cosine, sine_up, sine_down):
    return (
        lanes * cosine
        + pltpu.roll(lanes, ROT // 2, 1) * sine_up
        + pltpu.roll(lanes, LANES - ROT // 2, 1) * sine_down
    )


def stream(step, refs, held, sems):
    count = len(refs)
    copy = lambda k: pltpu.make_async_copy(refs[k], held.at[k % 2], sems.at[k % 2])

    @pl.when(step == 0)
    def _():
        copy(0).start()

    for k in range(1, count):

        @pl.when(step == k - 1)
        def _(k=k):
            copy(k).start()

    for k in range(count):

        @pl.when(step == k)
        def _(k=k):
            copy(k).wait()

    return held[lax.rem(step, 2)]


def one_buffer(shape):
    return pl.BlockSpec(
        shape, lambda *index: (0,) * len(shape), pipeline_mode=pl.Buffered(buffer_count=1)
    )


def stacked(shape):
    return pl.BlockSpec((1,) + shape, lambda i: (i, 0, 0))


def project_kernel(count, few, scale, *refs):
    x_refs = refs[:count]
    gain_ref, w_ref, cos_ref, up_ref, down_ref, a_ref, qkv_ref, held, sems = refs[count:]
    plain, _ = norm_parts(stream(pl.program_id(0), x_refs, held, sems).astype(fl))
    rows = (plain * gain_ref[...]).astype(bf)
    a_ref[0] = rows
    projected = matmul(rows, w_ref[:, : 3 * few])
    cosine, up, down = cos_ref[0], up_ref[0], down_ref[0]
    lane = lax.broadcasted_iota(jnp.int32, cosine.shape, 1)
    for start in range(0, 2 * few, LANES):
        turned = turn(projected[:, start : start + LANES], cosine, up, down)
        if start < few:
            turned = jnp.where(lane < few - start, turned * scale, turned)
        qkv_ref[0, :, start : start + LANES] = turned.astype(bf)
    qkv_ref[0, :, 2 * few :] = projected[:, 2 * few :].astype(bf)


def project(blocks, gain, weight, tables, scale, few):
    count = len(blocks)
    rows, width = blocks[0].shape
    used = -(-3 * few // LANES) * LANES
    return pl.pallas_call(
        functools.partial(project_kernel, count, few, scale),
        grid=(count,),
        in_specs=[pl.BlockSpec(memory_space=pl.ANY)] * count
        + [
            whole((1, width)),
            one_buffer((width, used)),
            stacked((rows, LANES)),
            stacked((rows, LANES)),
            stacked((rows, LANES)),
        ],
        out_specs=[stacked((rows, width)), stacked((rows, 3 * few))],
        out_shape=[
            jax.ShapeDtypeStruct((count, rows, width), bf),
            jax.ShapeDtypeStruct((count, rows, 3 * few), bf),
        ],
        scratch_shapes=[pltpu.VMEM((2, rows, width), bf), pltpu.SemaphoreType.DMA((2,))],
        compiler_params=params(48),
        cost_estimate=SHORT,
        name="project",
    )(*blocks, gain, weight, *(table.reshape(count, rows, LANES) for table in tables))


def marked(rows, mark):
    lane = lax.broadcasted_iota(jnp.int32, (rows.shape[0], LANES - HD), 1)
    more = jnp.where(lane == 0, mark, 0.0)
    return jnp.concatenate([rows.astype(fl), more], axis=1).astype(bf)


def attend_kernel(heads, wide, block, qkv_ref, mask_ref, o_ref, lse_ref):
    bias = jnp.where(mask_ref[:, 0:1] > 0.5, 0.0, masked_score)
    total = qkv_ref.shape[0]
    for h in range(heads):
        low, high = h * HD, (h + 1) * HD
        keys = marked(qkv_ref[:, wide + low : wide + high], bias)
        values_t = flip(qkv_ref[:, 2 * wide + low : 2 * wide + high]).astype(bf)
        for b in range(total // block):
            queries = marked(qkv_ref[b * block : (b + 1) * block, low:high], 1.0)
            scores = matmul_t(keys, queries)
            peak = jnp.max(scores, axis=0, keepdims=True)
            weights = jnp.exp(scores - peak)
            sums = jnp.sum(weights, axis=0, keepdims=True)
            mixed = matmul(values_t, weights.astype(bf)) / sums
            o_ref[b * block : (b + 1) * block, low:high] = mixed.T.astype(bf)
            spot = h * (total // block) + b
            lse_ref[0, spot : spot + 1, :] = peak + jnp.log(sums)


def attend(qkv, mask, latents, heads, block):
    rows, lanes = qkv.shape
    wide = lanes // 3
    total = rows // latents
    spots = heads * (total // block)
    spots_up = -(-spots // 8) * 8
    return pl.pallas_call(
        functools.partial(attend_kernel, heads, wide, block),
        grid=(latents,),
        in_specs=[
            pl.BlockSpec((total, lanes), lambda i: (i, 0)),
            pl.BlockSpec((total, LANES), lambda i: (i, 0)),
        ],
        out_specs=[
            pl.BlockSpec((total, wide), lambda i: (i, 0)),
            pl.BlockSpec((1, spots_up, block), lambda i: (i, 0, 0)),
        ],
        out_shape=[
            jax.ShapeDtypeStruct((rows, wide), bf),
            jax.ShapeDtypeStruct((latents, spots_up, block), fl),
        ],
        compiler_params=params(48),
        cost_estimate=SHORT,
        name="attend",
    )(qkv, mask)


def attend_back_kernel(
    heads, wide, block, scale, qkv_ref, do_ref, o_ref, lse_ref, mask_ref, cos_ref, up_ref, down_ref,
    out_ref, work_ref,
):
    bias = jnp.where(mask_ref[:, 0:1] > 0.5, 0.0, masked_score)
    total = qkv_ref.shape[0]
    ones = jnp.ones((8, HD), fl)
    for h in range(heads):
        low, high = h * HD, (h + 1) * HD
        keys = qkv_ref[:, wide + low : wide + high]
        keys_t = flip(keys).astype(bf)
        keys = marked(keys, bias)
        values = qkv_ref[:, 2 * wide + low : 2 * wide + high]
        grad_keys = jnp.zeros((total, HD), fl)
        grad_values = jnp.zeros((total, HD), fl)
        for b in range(total // block):
            queries = qkv_ref[b * block : (b + 1) * block, low:high]
            grads = do_ref[b * block : (b + 1) * block, low:high]
            mixed = o_ref[b * block : (b + 1) * block, low:high]
            spot = h * (total // block) + b
            scores = matmul_t(keys, marked(queries, 1.0))
            probs = jnp.exp(scores - lse_ref[0, spot : spot + 1, :])
            delta = lax.dot_general(
                ones,
                grads.astype(fl) * mixed.astype(fl),
                (((1,), (1,)), ((), ())),
                precision=lax.Precision.HIGHEST,
                preferred_element_type=fl,
            )[0:1]
            grad_scores = (probs * (matmul_t(values, grads) - delta)).astype(bf)
            grad_values += matmul(probs.astype(bf), grads)
            grad_keys += matmul(grad_scores, queries)
            grad_queries = matmul(keys_t, grad_scores) * scale
            work_ref[b * block : (b + 1) * block, low:high] = grad_queries.T
        work_ref[:, wide + low : wide + high] = grad_keys
        work_ref[:, 2 * wide + low : 2 * wide + high] = grad_values
    cosine, up, down = cos_ref[...], -up_ref[...], -down_ref[...]
    for start in range(0, 2 * wide, LANES):
        out_ref[:, start : start + LANES] = turn(
            work_ref[:, start : start + LANES], cosine, up, down
        ).astype(bf)
    out_ref[:, 2 * wide :] = work_ref[:, 2 * wide :].astype(bf)


def attend_back(qkv, grads, mixed, lse, mask, tables, latents, heads, block, scale):
    rows, lanes = qkv.shape
    wide = lanes // 3
    total = rows // latents
    by_latent = lambda n: pl.BlockSpec((total, n), lambda i: (i, 0))
    return pl.pallas_call(
        functools.partial(attend_back_kernel, heads, wide, block, scale),
        grid=(latents,),
        in_specs=[
            by_latent(lanes),
            by_latent(wide),
            by_latent(wide),
            pl.BlockSpec((1,) + lse.shape[1:], lambda i: (i, 0, 0)),
            by_latent(LANES),
            by_latent(LANES),
            by_latent(LANES),
            by_latent(LANES),
        ],
        out_specs=by_latent(lanes),
        out_shape=jax.ShapeDtypeStruct((rows, lanes), bf),
        scratch_shapes=[pltpu.VMEM((total, lanes), fl)],
        compiler_params=params(56),
        cost_estimate=SHORT,
        name="attend_back",
    )(qkv, grads, mixed, lse, mask, *tables)


def cross_kernel(heads, scale, q_ref, kv_ref, mask_ref, o_ref, lse_ref):
    mask = mask_ref[0, :, 0:1] > 0.5
    wide = heads * HD
    for first in range(0, heads, 2):
        pair = []
        for h in (first, first + 1):
            low, high = h * HD, (h + 1) * HD
            keys = kv_ref[0, :, low:high]
            values_t = flip(kv_ref[0, :, wide + low : wide + high]).astype(bf)
            scores = jnp.where(mask, matmul_t(keys, q_ref[0, :, low:high]) * scale, masked_score)
            peak = jnp.max(scores, axis=0, keepdims=True)
            weights = jnp.exp(scores - peak)
            sums = jnp.sum(weights, axis=0, keepdims=True)
            pair.append(matmul(values_t, weights.astype(bf)) / sums)
            lse_ref[0, h : h + 1, :] = peak + jnp.log(sums)
        o_ref[0, :, first * HD : (first + 2) * HD] = (
            jnp.concatenate(pair, axis=0).T.astype(bf)
        )


def cross(queries, pairs, mask, scale):
    latents, rows, wide = queries.shape
    heads = wide // HD
    heads_up = -(-heads // 8) * 8
    one = lambda shape: pl.BlockSpec((1,) + shape, lambda i: (i, 0, 0))
    return pl.pallas_call(
        functools.partial(cross_kernel, heads, scale),
        grid=(latents,),
        in_specs=[one((rows, wide)), one(pairs.shape[1:]), one(mask.shape[1:])],
        out_specs=[one((rows, wide)), one((heads_up, rows))],
        out_shape=[
            jax.ShapeDtypeStruct((latents, rows, wide), bf),
            jax.ShapeDtypeStruct((latents, heads_up, rows), fl),
        ],
        compiler_params=params(32),
        cost_estimate=SHORT,
        name="cross",
    )(queries, pairs, mask)


def cross_back_kernel(
    heads, scale, q_ref, kv_ref, do_ref, o_ref, lse_ref, mask_ref, dq_ref, dkv_ref
):
    mask = mask_ref[0, :, 0:1] > 0.5
    wide = heads * HD
    ones = jnp.ones((8, HD), fl)
    for first in range(0, heads, 2):
        pair = []
        grad_keys = []
        grad_values = []
        for h in (first, first + 1):
            low, high = h * HD, (h + 1) * HD
            keys = kv_ref[0, :, low:high]
            keys_t = flip(keys).astype(bf)
            values = kv_ref[0, :, wide + low : wide + high]
            queries = q_ref[0, :, low:high]
            grads = do_ref[0, :, low:high]
            scores = jnp.where(mask, matmul_t(keys, queries) * scale, masked_score)
            probs = jnp.exp(scores - lse_ref[0, h : h + 1, :])
            delta = lax.dot_general(
                ones,
                grads.astype(fl) * o_ref[0, :, low:high].astype(fl),
                (((1,), (1,)), ((), ())),
                precision=lax.Precision.HIGHEST,
                preferred_element_type=fl,
            )[0:1]
            grad_scores = (probs * (matmul_t(values, grads) - delta)).astype(bf)
            grad_values.append(matmul(probs.astype(bf), grads))
            grad_keys.append(matmul(grad_scores, queries) * scale)
            pair.append(matmul(keys_t, grad_scores) * scale)
        low, high = first * HD, (first + 2) * HD
        dq_ref[0, :, low:high] = jnp.concatenate(pair, axis=0).T.astype(bf)
        dkv_ref[0, :, low:high] = jnp.concatenate(grad_keys, axis=1).astype(bf)
        dkv_ref[0, :, wide + low : wide + high] = jnp.concatenate(grad_values, axis=1).astype(bf)


def cross_back(queries, pairs, grads, mixed, lse, mask, scale):
    latents, rows, wide = queries.shape
    heads = wide // HD
    one = lambda shape: pl.BlockSpec((1,) + shape, lambda i: (i, 0, 0))
    return pl.pallas_call(
        functools.partial(cross_back_kernel, heads, scale),
        grid=(latents,),
        in_specs=[
            one((rows, wide)),
            one(pairs.shape[1:]),
            one((rows, wide)),
            one((rows, wide)),
            one(lse.shape[1:]),
            one(mask.shape[1:]),
        ],
        out_specs=[one((rows, wide)), one(pairs.shape[1:])],
        out_shape=[
            jax.ShapeDtypeStruct(queries.shape, bf),
            jax.ShapeDtypeStruct(pairs.shape, bf),
        ],
        compiler_params=params(32),
        cost_estimate=SHORT,
        name="cross_back",
    )(queries, pairs, grads, mixed, lse, mask)


def mix_back_kernel(count, *refs):
    g_refs = refs[:count]
    w_ref, o_ref, do_ref, grad_ref, held, total, sems = refs[count:]
    step = pl.program_id(0)
    few = o_ref.shape[2]

    @pl.when(step == 0)
    def _():
        total[...] = jnp.zeros_like(total)

    rows = stream(step, g_refs, held, sems)
    do_ref[0] = matmul(rows, w_ref[:, :few]).astype(bf)
    total[...] += matmul(flip(o_ref[0]).astype(bf), rows)

    @pl.when(step == count - 1)
    def _():
        grad_ref[...] = total[...].T.astype(bf)


def mix_back(blocks, weight, mixed):
    count = len(blocks)
    rows, width = blocks[0].shape
    few = mixed.shape[2]
    return pl.pallas_call(
        functools.partial(mix_back_kernel, count),
        grid=(count,),
        in_specs=[pl.BlockSpec(memory_space=pl.ANY)] * count
        + [one_buffer(weight.shape), stacked((rows, few))],
        out_specs=[stacked((rows, few)), whole((width, few))],
        out_shape=[
            jax.ShapeDtypeStruct((count, rows, few), bf),
            jax.ShapeDtypeStruct((width, few), bf),
        ],
        scratch_shapes=[
            pltpu.VMEM((2, rows, width), bf),
            pltpu.VMEM((few, width), fl),
            pltpu.SemaphoreType.DMA((2,)),
        ],
        compiler_params=params(48),
        cost_estimate=SHORT,
        name="mix_back",
    )(*blocks, weight, mixed)


def fetched(shape):
    return shape[2] % 16 == 0 and shape[3] % LANES == 0


def mlp_kernel(count, given, *refs):
    a_refs, dy_refs = refs[:given], refs[given : 2 * given]
    (
        gate_ref,
        up_ref,
        down_ref,
        a_ref,
        dy_ref,
        h_ref,
        dgu_ref,
        out_other,
        out_own,
        da_other,
        da_own,
        weight,
        a_held,
        dy_held,
        weight_sems,
        block_sems,
    ) = refs[2 * given :]
    step = pl.program_id(0)
    ctxs, shards, owned, units = gate_ref.shape

    def weight_copies():
        for k, kind in enumerate((gate_ref, up_ref, down_ref)):
            for c in range(ctxs):
                for s in range(shards):
                    row = (s * ctxs + c) * owned
                    yield pltpu.make_async_copy(
                        kind.at[c, s],
                        weight.at[pl.ds(row, owned), pl.ds(k * units, units)],
                        weight_sems.at[k, c * shards + s],
                    )

    def block_copies(k):
        for side, (sources, held) in enumerate(((a_refs, a_held), (dy_refs, dy_held))):
            source = sources[k] if given == count else sources[0].at[k]
            yield pltpu.make_async_copy(source, held.at[k % 2], block_sems.at[side, k % 2])

    @pl.when(step == 0)
    def _():
        for copy in block_copies(0):
            copy.start()
        if fetched(gate_ref.shape):
            for copy in weight_copies():
                copy.start()

    for k in range(1, count):

        @pl.when(step == k - 1)
        def _(k=k):
            for copy in block_copies(k):
                copy.start()

    for k in range(count):

        @pl.when(step == k)
        def _(k=k):
            for copy in block_copies(k):
                copy.wait()

    @pl.when(step == 0)
    def _():
        if fetched(gate_ref.shape):
            for copy in weight_copies():
                copy.wait()
        else:
            for s in range(shards):
                for c in range(ctxs):
                    row = (s * ctxs + c) * owned
                    for k, kind in enumerate((gate_ref, up_ref, down_ref)):
                        weight[row : row + owned, k * units : (k + 1) * units] = kind[c, s]

    slot = lax.rem(step, 2)
    rows = a_held[slot]
    grads = dy_held[slot]
    a_ref[0] = rows
    dy_ref[0] = grads
    gate = matmul(rows, weight[:, :units])
    upward = matmul(rows, weight[:, units : 2 * units])
    sigmoid = jax.nn.sigmoid(gate)
    activated = gate * sigmoid
    hidden = (activated * upward).astype(bf)
    h_ref[0] = hidden
    grad_hidden = matmul(grads, weight[:, 2 * units :])
    grad_gate = (grad_hidden * upward * sigmoid * (1.0 + gate * (1.0 - sigmoid))).astype(bf)
    grad_up = (grad_hidden * activated).astype(bf)
    dgu_ref[0, :, :units] = grad_gate
    dgu_ref[0, :, units:] = grad_up
    da = (
        matmul_t(grad_gate, weight[:, :units]) + matmul_t(grad_up, weight[:, units : 2 * units])
    ).astype(bf)
    out = matmul_t(hidden, weight[:, 2 * units :]).astype(bf)

    @pl.when(step < count // 2)
    def _():
        da_other[0] = da
        out_other[0] = out

    @pl.when(step >= count // 2)
    def _():
        da_own[0] = da
        out_own[0] = out


def mlp(blocks, grads, weights):
    count = len(blocks)
    half = count // 2
    rows, width = blocks[0].shape
    units = weights[0].shape[3]
    if count > MOST_BLOCKS:
        blocks, grads = [jnp.stack(blocks)], [jnp.stack(grads)]
    given = len(blocks)
    ctxs, shards = weights[0].shape[:2]
    first = pl.BlockSpec((1, rows, width), lambda i: (jnp.minimum(i, half - 1), 0, 0))
    second = pl.BlockSpec((1, rows, width), lambda i: (jnp.maximum(i - half, 0), 0, 0))
    return pl.pallas_call(
        functools.partial(mlp_kernel, count, given),
        grid=(count,),
        in_specs=[pl.BlockSpec(memory_space=pl.ANY)] * (2 * given)
        + [
            pl.BlockSpec(memory_space=pl.ANY)
            if fetched(weights[0].shape)
            else one_buffer(weights[0].shape)
        ]
        * 3,
        out_specs=[
            stacked((rows, width)),
            stacked((rows, width)),
            stacked((rows, units)),
            stacked((rows, 2 * units)),
            first,
            second,
            first,
            second,
        ],
        out_shape=[
            jax.ShapeDtypeStruct((count, rows, width), bf),
            jax.ShapeDtypeStruct((count, rows, width), bf),
            jax.ShapeDtypeStruct((count, rows, units), bf),
            jax.ShapeDtypeStruct((count, rows, 2 * units), bf),
        ]
        + [jax.ShapeDtypeStruct((half, rows, width), bf)] * 4,
        scratch_shapes=[
            pltpu.VMEM((width, 3 * units), bf),
            pltpu.VMEM((2, rows, width), bf),
            pltpu.VMEM((2, rows, width), bf),
            pltpu.SemaphoreType.DMA((3, ctxs * shards)),
            pltpu.SemaphoreType.DMA((2, 2)),
        ],
        compiler_params=params(48),
        cost_estimate=SHORT,
        name="mlp",
    )(*blocks, *grads, *weights)


def after(value, *others):
    return lax.optimization_barrier((value,) + others)[0] if others else value


def swap(value):
    return lax.ppermute(value, "tp", [(0, 1), (1, 0)])


def ring_shift(value, by):
    size = lax.axis_size("ctx")
    return lax.ppermute(value, "ctx", [(i, (i - by) % size) for i in range(size)])


def cross_over(value, bits):
    size = lax.axis_size("shard")
    return lax.ppermute(value, "shard", [(i, i ^ bits) for i in range(size)])


def together(values, *others):
    return lax.optimization_barrier((tuple(values),) + others)[0]


def nothing(token):
    return ()


def ring_gather(own, first=(), second=()):
    size = lax.axis_size("ctx")
    if size != 4:
        return [own] + [after(ring_shift(own, r), *second) for r in range(1, size)]
    half = own.shape[-1] // 2
    following, before = together((ring_shift(own, 1), ring_shift(own, -1)), *first)
    far = together(
        (ring_shift(following[:, :half], 1), ring_shift(before[:, half:], -1)), *second
    )
    return [own, following, jnp.concatenate(far, axis=-1), before]


def ring_scatter(parts, first=(), between=nothing):
    if lax.axis_size("ctx") != 4:
        total = parts[0].astype(fl)
        for r in range(1, len(parts)):
            total = total + after(ring_shift(parts[r], -r), *between(parts[0])).astype(fl)
        return total
    half = parts[0].shape[-1] // 2
    by_after, by_before = together(
        (ring_shift(parts[2][:, :half], -1), ring_shift(parts[2][:, half:], 1)), *first
    )
    to_after = jnp.concatenate([parts[1][:, :half] + by_after, parts[1][:, half:]], axis=-1)
    to_before = jnp.concatenate([parts[3][:, :half], parts[3][:, half:] + by_before], axis=-1)
    from_before, from_after = together(
        (ring_shift(to_after, -1), ring_shift(to_before, 1)), *between(by_after)
    )
    return parts[0].astype(fl) + from_before.astype(fl) + from_after.astype(fl)


def ring_exchange(parts, before=()):
    return [parts[0]] + [after(ring_shift(part, -r), *before) for r, part in enumerate(parts[1:], 1)]


def square_exchange(parts, before=()):
    return [parts[0]] + [after(cross_over(part, r), *before) for r, part in enumerate(parts[1:], 1)]


def summed(parts):
    total = parts[0].astype(fl)
    for part in parts[1:]:
        total = total + part.astype(fl)
    return total


def at(array, index):
    return lax.dynamic_index_in_dim(array, index, 0, keepdims=False)


def rows_at(array, index, count):
    return lax.dynamic_slice_in_dim(array, index * count, count, 0)


def place(blocks, indices):
    out = jnp.zeros((len(blocks),) + blocks[0].shape, blocks[0].dtype)
    for block, index in zip(blocks, indices):
        out = lax.dynamic_update_index_in_dim(out, block, index, 0)
    return out


def square_gather(own, first=(), second=()):
    size = lax.axis_size("shard")
    if size != 4:
        return [own] + [after(cross_over(own, r), *second) for r in range(1, size)]
    half = own.shape[-1] // 2
    one, two = together((cross_over(own, 1), cross_over(own, 2)), *first)
    three = together((cross_over(two[:, :half], 1), cross_over(one[:, half:], 2)), *second)
    return [own, one, two, jnp.concatenate(three, axis=-1)]


def square_scatter(parts, first=(), between=nothing):
    size = lax.axis_size("shard")
    if size != 4:
        total = parts[0].astype(fl)
        for r in range(1, size):
            total = total + after(cross_over(parts[r], r), *between(parts[0])).astype(fl)
        return total
    half = parts[0].shape[-1] // 2
    by_one, by_two = together(
        (cross_over(parts[3][:, :half], 1), cross_over(parts[3][:, half:], 2)), *first
    )
    to_two = jnp.concatenate([parts[2][:, :half] + by_one, parts[2][:, half:]], axis=-1)
    to_one = jnp.concatenate([parts[1][:, :half], parts[1][:, half:] + by_two], axis=-1)
    from_one, from_two = together(
        (cross_over(to_one, 1), cross_over(to_two, 2)), *between(by_one)
    )
    return parts[0].astype(fl) + from_one.astype(fl) + from_two.astype(fl)


def total_over_all(value):
    for axis in ("tp", "shard", "ctx"):
        size = lax.axis_size(axis)
        bit = 1
        while bit < size:
            value = value + lax.ppermute(value, axis, [(i, i ^ bit) for i in range(size)])
            bit *= 2
    return value


def adam_step(weight, moment, square, grad, scale, decay, rate):
    grad = grad * scale
    moment_new = beta_first * moment + (1.0 - beta_first) * grad
    square_new = beta_second * square + (1.0 - beta_second) * grad * grad
    moment_hat = moment_new / (1.0 - beta_first**STEP)
    square_hat = square_new / (1.0 - beta_second**STEP)
    weight_new = weight - rate * (moment_hat / (jnp.sqrt(square_hat) + adam_eps) + decay * weight)
    return (moment_new, square_new, weight_new)


def rotary_tables(positions):
    lane = jnp.arange(LANES, dtype=jnp.int32) % HD
    step = (lane % (ROT // 2)).astype(fl) * 2.0 / ROT
    frequency = jnp.where(lane < ROT, 10000.0 ** (-step), 0.0)
    angles = positions.astype(fl)[:, None] * frequency[None, :]
    sine = jnp.sin(angles)
    up = jnp.where((lane >= ROT // 2) & (lane < ROT), sine, 0.0)
    down = jnp.where(lane < ROT // 2, -sine, 0.0)
    return (jnp.cos(angles), up, down)


def local(
    tokens,
    conditioning,
    cotangent,
    piece_lengths,
    start_positions,
    cond_counts,
    norm_gains,
    gains_moment,
    gains_square,
    qkv_weight,
    qkv_moment,
    qkv_square,
    output_weight,
    output_moment,
    output_square,
    cross_query_weight,
    cross_query_moment,
    cross_query_square,
    cross_pair_weight,
    cross_pair_moment,
    cross_pair_square,
    cross_out_weight,
    cross_out_moment,
    cross_out_square,
    gate_up_weight,
    gate_up_moment,
    gate_up_square,
    down_weight,
    down_moment,
    down_square,
):
    seqs, cap, width = tokens.shape
    cond_len = conditioning.shape[1]
    pieces = piece_lengths.shape[1]
    scale = HD ** (-0.5)
    shards = lax.axis_size("shard")
    ctxs = lax.axis_size("ctx")
    shard_index = lax.axis_index("shard")
    ctx_index = lax.axis_index("ctx")
    tp_index = lax.axis_index("tp")
    owned = qkv_weight.shape[0]
    local_width = qkv_weight.shape[2]
    units_half = down_weight.shape[1]
    few = local_width // ctxs
    heads_few = few // HD
    units = units_half // shards

    latent_order = (tp_index + jnp.arange(seqs, dtype=jnp.int32)) % seqs
    piece_order = (ctx_index + jnp.arange(pieces, dtype=jnp.int32)) % pieces
    mine = lambda array: lax.dynamic_index_in_dim(array, latent_order[0], 0, keepdims=False)
    others = lambda array: lax.dynamic_index_in_dim(array, latent_order[1], 0, keepdims=False)

    def both(array):
        return jnp.stack([mine(array), others(array)])

    offsets = jnp.cumsum(piece_lengths, axis=1) - piece_lengths
    slot = jnp.arange(cap, dtype=jnp.int32)
    lengths_here = both(piece_lengths)[:, piece_order]
    offsets_here = both(offsets)[:, piece_order]
    starts_here = both(start_positions)
    positions = (starts_here[:, None, None] + offsets_here[:, :, None] + slot).reshape(-1)
    key_valid = (slot < lengths_here[:, :, None]).reshape(-1)
    key_mask = jnp.broadcast_to(key_valid.astype(fl)[:, None], (key_valid.shape[0], LANES))
    tables = lax.optimization_barrier(rotary_tables(positions))
    other_valid = (slot < lengths_here[1, 0]).astype(fl)[:, None]
    own_valid = (slot < lengths_here[0, 0]).astype(fl)[:, None]

    tokens_mine = mine(tokens)
    tokens_other = others(tokens)
    dy_mine = mine(cotangent).astype(fl) * own_valid
    dy_low = dy_mine.astype(bf)

    kinds = jnp.concatenate(
        [
            qkv_weight.astype(bf),
            output_weight.astype(bf)[:, None],
            cross_pair_weight.astype(bf),
        ],
        axis=1,
    )
    n_kinds = kinds.shape[1]
    kinds = jnp.transpose(kinds.reshape(owned, n_kinds, ctxs, few), (2, 0, 1, 3)).reshape(
        ctxs, owned, n_kinds * few
    )
    gain_lanes = jnp.pad(jnp.transpose(norm_gains).astype(bf), ((0, 0), (0, LANES - 3)))
    sent_attn = jnp.concatenate(
        [kinds, jnp.broadcast_to(gain_lanes[None], (ctxs, owned, LANES))], axis=2
    )
    sent_attn = after(sent_attn, tokens_mine)
    ctx_after = [(ctx_index + r) % ctxs for r in range(ctxs)]
    ctx_before = [(ctx_index - r) % ctxs for r in range(ctxs)]
    shard_near = [shard_index ^ r for r in range(shards)]
    sent_mlp = jnp.concatenate(
        [
            gate_up_weight.astype(bf),
            down_weight.astype(bf)[:, None],
        ],
        axis=1,
    )
    sent_mlp = jnp.transpose(sent_mlp.reshape(owned, 3, shards, units), (2, 0, 1, 3)).reshape(
        shards, owned, 3 * units
    )
    attn_rows = after(
        lax.all_to_all(sent_attn, "ctx", 0, 0, tiled=True), sent_mlp, *tables
    ).reshape(ctxs * owned, -1)
    attn_full = lax.all_gather(attn_rows, "shard", axis=0, tiled=True)
    pair_full = attn_full[:, 4 * few : 6 * few]
    output_full = attn_full[:, 3 * few : 4 * few]
    gains = jnp.transpose(attn_full[:, n_kinds * few : n_kinds * few + 3].astype(fl))

    token_blocks = ring_gather(tokens_mine, (attn_rows,))
    sent_mlp = lax.all_to_all(sent_mlp, "shard", 0, 0, tiled=True)
    sent_gate, sent_up, sent_down = (
        sent_mlp[:, :, k * units : (k + 1) * units] for k in range(3)
    )
    over_ctx = lambda array: lax.all_gather(array, "ctx", axis=0, tiled=False)
    token_swapped = [tokens_other] + [swap(block) for block in token_blocks[1:]]
    token_last = after(token_swapped[-1], sent_gate, sent_up, sent_down)

    total = pieces * cap
    block = total // 3
    input1, qkv = project(
        token_blocks + token_swapped[:-1] + [token_last], gains[0:1], attn_full, tables, scale, few
    )
    qkv = qkv.reshape(seqs * total, 3 * few)
    cond_up = -(-cond_len // 16) * 16
    cond_rows = jnp.pad(both(conditioning), ((0, 0), (0, cond_up - cond_len), (0, 0))).reshape(
        seqs * cond_up, width
    )
    own_pairs = matmul(cond_rows, pair_full).astype(bf)
    gate_full = over_ctx(after(sent_gate, token_last, attn_full))
    sent_cross = jnp.concatenate(
        [cross_query_weight.astype(bf), cross_out_weight.astype(bf)], axis=1
    )
    sent_cross = after(sent_cross, qkv)
    cross_rows = [sent_cross] + [ring_shift(sent_cross, r) for r in range(1, ctxs)]
    mixed_low, lse = attend(qkv, key_mask, seqs, heads_few, block)
    cross_rows = place(cross_rows, ctx_after).reshape(ctxs * owned, -1)
    cross_full = lax.all_gather(after(cross_rows, gate_full), "shard", axis=0, tiled=True)
    partial = matmul_t(mixed_low, output_full).astype(bf).reshape(seqs, pieces, cap, width)
    from_other = swap(partial[1])
    mine_parts = [partial[0, r] + from_other[r] for r in range(pieces)]
    own_pairs = after(own_pairs, mixed_low)
    pairs = [own_pairs] + [ring_shift(own_pairs, r) for r in range(1, ctxs)]
    pairs = place(pairs, ctx_after)
    pairs = jnp.transpose(
        pairs.reshape(ctxs, seqs, cond_up, 2, few), (1, 2, 3, 0, 4)
    ).reshape(seqs, cond_up, 2 * local_width)
    query_full = cross_full[:, :local_width]
    cross_out_full = cross_full[:, local_width:]
    x_rows = tokens_mine.astype(fl)
    x_first = x_rows + ring_scatter(mine_parts, (cross_rows,), lambda token: (pairs,))
    up_full = over_ctx(after(sent_up, x_first))
    down_full = over_ctx(after(sent_down, x_first))
    dy_low = after(dy_low, x_first)
    dy_blocks = [dy_low] + [cross_over(dy_low, r) for r in range(1, shards)]
    dy_other = (others(cotangent).astype(fl) * other_valid).astype(bf)
    dy_swapped = [dy_other] + [swap(block_of) for block_of in dy_blocks[1:]]

    plain2, inverse2 = norm_parts(x_first)
    input2_mine = (plain2 * gains[1]).astype(bf)
    input2 = jnp.concatenate([input2_mine, swap(input2_mine)], axis=0)
    cross_queries = matmul(input2, query_full).astype(bf).reshape(seqs, cap, local_width)
    cond_valid = jnp.arange(cond_up, dtype=jnp.int32)[None, :] < both(cond_counts)[:, None]
    cond_mask = jnp.broadcast_to(cond_valid.astype(fl)[:, :, None], (seqs, cond_up, LANES))
    cross_low, cross_lse = cross(cross_queries, pairs, cond_mask, scale)
    cross_low_rows = cross_low.reshape(seqs * cap, local_width)
    cross_partial = matmul_t(cross_low_rows, cross_out_full).astype(bf)
    x_second = x_first + (
        cross_partial[:cap].astype(fl) + swap(cross_partial[cap:]).astype(fl)
    )

    plain3, inverse3 = norm_parts(x_second)
    input3 = (plain3 * gains[2]).astype(bf)
    input3_blocks = square_gather(input3, (), dy_swapped)
    (
        input3_all,
        dy_all,
        hidden,
        grad_gated,
        down_other,
        down_own,
        back_other,
        back_own,
    ) = mlp(
        [swap(block_of) for block_of in input3_blocks] + input3_blocks,
        dy_swapped + dy_blocks,
        (gate_full, up_full, down_full),
    )
    merged = lambda array: array.reshape(-1, array.shape[-1])
    grad_down = contract_rows(merged(dy_all), merged(hidden)).astype(bf)
    grad_gate = contract_rows(merged(input3_all), merged(grad_gated)[:, :units]).astype(bf)
    grad_up = contract_rows(merged(input3_all), merged(grad_gated)[:, units:]).astype(bf)

    def add_cores(own, other):
        from_other = swap(other)
        return [own[r] + from_other[r] for r in range(own.shape[0])]

    def by_owner(array):
        return jnp.transpose(
            array.reshape(shards, ctxs, owned, array.shape[1]), (1, 0, 2, 3)
        ).reshape(ctxs * shards * owned, -1)

    def sum_over_ctx(array):
        return lax.psum_scatter(array, "ctx", scatter_dimension=0, tiled=True)

    grad_down, grad_gate, grad_up = by_owner(grad_down), by_owner(grad_gate), by_owner(grad_up)
    back_sum = square_scatter(
        add_cores(back_own, back_other), (grad_down,), lambda token: (grad_gate, grad_up)
    )
    back3, grad_gain3 = norm_back(back_sum, plain3, inverse3, gains[2])

    def natural(first, second):
        straight = tp_index == 0
        return jnp.stack(
            [jnp.where(straight, first, second), jnp.where(straight, second, first)]
        )

    sum_down = sum_over_ctx(grad_down)
    sum_gate = sum_over_ctx(grad_gate)

    grad_second = dy_mine + back3
    grad2_mine = grad_second.astype(bf)
    grad2_low = jnp.concatenate([grad2_mine, swap(grad2_mine)], axis=0)
    grad_cross_out = contract_rows(grad2_low, cross_low_rows)
    grad_cmixed = matmul(grad2_low, cross_out_full).astype(bf).reshape(seqs, cap, local_width)
    grad_cq, grad_pairs = cross_back(
        cross_queries, pairs, grad_cmixed, cross_low, cross_lse, cond_mask, scale
    )
    grad_cq = grad_cq.reshape(seqs * cap, local_width)
    grad_query = contract_rows(input2, grad_cq)
    query_partial = matmul_t(grad_cq, query_full).astype(bf)
    back2, grad_gain2 = norm_back(
        query_partial[:cap].astype(fl) + swap(query_partial[cap:]).astype(fl),
        plain2,
        inverse2,
        gains[1],
    )
    grad_cross = jnp.concatenate([grad_query.astype(bf), grad_cross_out.astype(bf)], axis=1)
    grad_pairs = jnp.transpose(
        grad_pairs.reshape(seqs, cond_up, 2, ctxs, few), (3, 0, 1, 2, 4)
    ).reshape(ctxs, seqs * cond_up, 2 * few)

    grad_first = grad_second + back2
    grad1_mine = grad_first.astype(bf)
    down_parts = add_cores(after(down_own, back_sum), after(down_other, back_sum))
    down_sum = summed(square_exchange(down_parts, (grad1_mine,)))
    block_mine = (x_second + down_sum).astype(bf)
    block_out = natural(block_mine, swap(block_mine))
    grad1_blocks = ring_gather(
        grad1_mine, (grad_cross, grad_pairs, sum_down), (block_mine, sum_gate)
    )
    cross_sum = lax.psum_scatter(
        after(grad_cross, grad1_mine), "shard", scatter_dimension=0, tiled=True
    )
    grad_mixed, grad_output = mix_back(
        grad1_blocks + [swap(block_of) for block_of in grad1_blocks],
        output_full,
        mixed_low.reshape(seqs * pieces, cap, few),
    )
    sum_up = sum_over_ctx(after(grad_up, grad1_blocks[2]))
    grad_pairs = after(grad_pairs, grad_mixed)
    own_pair_grads = summed(
        ring_exchange([at(grad_pairs, index) for index in ctx_after])
    ).astype(bf)
    grad_pair = contract_rows(cond_rows, own_pair_grads).astype(bf)
    to_owner = lambda array: jnp.transpose(
        lax.all_to_all(array.reshape(shards, owned, -1), "shard", 0, 0, tiled=True), (1, 0, 2)
    ).reshape(owned, units_half)
    own_gate = to_owner(after(sum_gate, grad_mixed))
    own_down = to_owner(after(sum_down, grad_mixed))
    grad_projected = attend_back(
        qkv,
        grad_mixed.reshape(seqs * total, few),
        mixed_low,
        lse,
        key_mask,
        tables,
        seqs,
        heads_few,
        block,
        scale,
    )
    grad_turned = after(grad_projected, own_gate, own_down, grad_pair, cross_sum)
    grad_qkv = contract_rows(merged(input1), grad_turned).astype(bf)
    grad_attn = jnp.concatenate([grad_qkv, grad_output, grad_pair], axis=1)
    attn_sum = lax.psum_scatter(grad_attn, "shard", scatter_dimension=0, tiled=True)
    first_partial = matmul_t(after(grad_turned, grad_attn, sum_up), attn_full[:, : 3 * few]).astype(
        bf
    ).reshape(seqs, pieces, cap, width)
    first_parts = add_cores(first_partial[0], first_partial[1])
    arrived = []

    def exchange(token):
        arrived.extend(
            [
                to_owner(after(sum_up, token)),
                summed(
                    ring_exchange(
                        [rows_at(after(cross_sum, token), index, owned) for index in ctx_after]
                    )
                ),
            ]
        )
        return arrived

    back1_sum = ring_scatter(first_parts, (), exchange)
    own_up = arrived[0]
    own_cross = arrived[1]
    plain1, inverse1 = norm_parts(x_rows)
    back1, grad_gain1 = norm_back(back1_sum, plain1, inverse1, gains[0])
    tokens_grad_mine = grad_first + back1
    tokens_grad = natural(tokens_grad_mine, swap(tokens_grad_mine))

    own_kinds = lax.all_to_all(attn_sum.reshape(ctxs, owned, -1), "ctx", 0, 0, tiled=True)
    own_kinds = jnp.transpose(
        own_kinds.reshape(ctxs, owned, n_kinds, few), (1, 2, 0, 3)
    ).reshape(owned, n_kinds, local_width).astype(fl)
    own_qkv = own_kinds[:, :3]
    own_output = own_kinds[:, 3]
    own_pair = own_kinds[:, 4:]
    own_query = own_cross[:, :local_width]
    own_cross_out = own_cross[:, local_width:]
    own_gate_up = with_layout_constraint(
        jnp.stack([own_gate, own_up], axis=1), Layout((0, 1, 2))
    ).astype(fl)
    own_down = own_down.astype(fl)

    squares = jnp.sum(own_kinds * own_kinds) + jnp.sum(own_cross * own_cross)
    squares = squares + jnp.sum(own_gate_up * own_gate_up) + jnp.sum(own_down * own_down)
    totals = total_over_all(
        jnp.concatenate(
            [
                jnp.stack([grad_gain1, grad_gain2, grad_gain3]),
                jnp.broadcast_to(squares, (5, width)),
            ]
        )
    )
    gain_grads = totals[:3]
    own_gains = lax.dynamic_slice_in_dim(
        gain_grads, (shard_index * ctxs + ctx_index) * owned, owned, 1
    )
    grad_norm = jnp.sqrt(totals[3, 0] + jnp.sum(gain_grads * gain_grads))
    clip_scale = clip_norm / jnp.maximum(grad_norm, clip_norm)

    def step(weight, moment, square, grad):
        return adam_step(weight, moment, square, grad, clip_scale, weight_decay, learn_rate)

    return (
        block_out,
        tokens_grad,
        grad_norm,
        *adam_step(
            norm_gains, gains_moment, gains_square, own_gains, clip_scale, 0.0, gain_rate
        ),
        *step(qkv_weight, qkv_moment, qkv_square, own_qkv),
        *step(output_weight, output_moment, output_square, own_output),
        *step(cross_query_weight, cross_query_moment, cross_query_square, own_query),
        *step(cross_pair_weight, cross_pair_moment, cross_pair_square, own_pair),
        *step(cross_out_weight, cross_out_moment, cross_out_square, own_cross_out),
        *step(gate_up_weight, gate_up_moment, gate_up_square, own_gate_up),
        *step(down_weight, down_moment, down_square, own_down),
    )


def solution(mesh):
    in_specs = (
        P("shard", "ctx", None),
        P("shard", None, None),
        P("shard", "ctx", None),
        P("shard", None),
        P("shard"),
        P("shard"),
        P(None, ("shard", "ctx")),
        P(None, ("shard", "ctx")),
        P(None, ("shard", "ctx")),
        P(("shard", "ctx"), None, "tp"),
        P(("shard", "ctx"), None, "tp"),
        P(("shard", "ctx"), None, "tp"),
        P(("shard", "ctx"), "tp"),
        P(("shard", "ctx"), "tp"),
        P(("shard", "ctx"), "tp"),
        P(("shard", "ctx"), "tp"),
        P(("shard", "ctx"), "tp"),
        P(("shard", "ctx"), "tp"),
        P(("shard", "ctx"), None, "tp"),
        P(("shard", "ctx"), None, "tp"),
        P(("shard", "ctx"), None, "tp"),
        P(("shard", "ctx"), "tp"),
        P(("shard", "ctx"), "tp"),
        P(("shard", "ctx"), "tp"),
        P(("shard", "ctx"), None, "tp"),
        P(("shard", "ctx"), None, "tp"),
        P(("shard", "ctx"), None, "tp"),
        P(("shard", "ctx"), "tp"),
        P(("shard", "ctx"), "tp"),
        P(("shard", "ctx"), "tp"),
    )
    out_specs = (
        P("shard", "ctx", None),
        P("shard", "ctx", None),
        P(),
        P(None, ("shard", "ctx")),
        P(None, ("shard", "ctx")),
        P(None, ("shard", "ctx")),
        P(("shard", "ctx"), None, "tp"),
        P(("shard", "ctx"), None, "tp"),
        P(("shard", "ctx"), None, "tp"),
        P(("shard", "ctx"), "tp"),
        P(("shard", "ctx"), "tp"),
        P(("shard", "ctx"), "tp"),
        P(("shard", "ctx"), "tp"),
        P(("shard", "ctx"), "tp"),
        P(("shard", "ctx"), "tp"),
        P(("shard", "ctx"), None, "tp"),
        P(("shard", "ctx"), None, "tp"),
        P(("shard", "ctx"), None, "tp"),
        P(("shard", "ctx"), "tp"),
        P(("shard", "ctx"), "tp"),
        P(("shard", "ctx"), "tp"),
        P(("shard", "ctx"), None, "tp"),
        P(("shard", "ctx"), None, "tp"),
        P(("shard", "ctx"), None, "tp"),
        P(("shard", "ctx"), "tp"),
        P(("shard", "ctx"), "tp"),
        P(("shard", "ctx"), "tp"),
    )
    return jax.shard_map(local, mesh=mesh, in_specs=in_specs, out_specs=out_specs, check_vma=False)
```
